32 devices in a mesh: slab: 8 (over z, y), lat: 4 (over x, core).
Axes of the slice: x: 2, y: 2, z: 4, core: 2. Of those that a mesh axis runs over, the one named last changes fastest.
Arguments:
- residual_blocks: float32 [1024, 2, 64, 128], P(('slab', 'lat')), may hold values from -1.5 to 1.5
- residual_slab: int32 [1024, 1], P(('slab', 'lat')), may hold values from 0 to 7; in each aligned block of 32 rows (0 to 31, 32 to 63, ...) at most 4 rows name the same one
- residual_pos: int32 [1024], P(('slab', 'lat')), may hold values from 0 to 3
- shot_ids: int32 [64], replicated, may hold values from 0 to 63, each once
- wavelet: float32 [64, 2], replicated, may hold values from -4 to 4
- down_panel: float32 [8, 4, 2, 512, 512], P('slab', 'lat'), may hold values from -1 to 1
- up_panel: float32 [8, 4, 2, 512, 512], P('slab', 'lat'), may hold values from -1 to 1
- recovery: float32 [8, 4, 2, 768, 1024], P('slab', 'lat'), may hold values from -0.109375 to 0.109375
- forward_field: float32 [8, 4, 2, 64, 1024], P('slab', 'lat'), may hold values from -3 to 3
- element_owner: int32 [256, 1], P(('slab', 'lat')), may hold values from 0 to 7; in each aligned block of 8 rows (0 to 7, 8 to 15, ...) at most 2 rows name the same one
- element_slot: int32 [256], P(('slab', 'lat')), may hold values from 0 to 7
Outputs:
- adjoint_trace: float32 [8, 4, 2, 64, 512], P('slab', 'lat')
- velocity_gradient: float32 [8, 4, 8, 128], P('slab', 'lat')
The draws below stay inside these ranges and needn't reach their ends.
Inputs may be any that keep to these rules, and one draw needn't show every extreme that they name: `residual_slab`: in the 32 rows of one device no slab is named more than 4 times, a bound that some block reaches. `shot_ids`: each shot number appears once. `element_owner`: in the 8 rows of one device no slab is named more than 2 times, a bound that some block reaches.
All inputs are finite; a program needn't handle non-finite values.
Results may differ from the reference program's by a relative error of at most 0.00014.
Values sent between devices are 32-bit elements; how exact they have to be, the bound alone decides.
No kernel may reach another device: no remote copies, remote signals or barrier semaphores. Data moves between devices by JAX's collectives and lax.ppermute only.
A program may use at most 128 MiB of HBM per device.

```python
import math
import jax
import jax.numpy as jnp
import numpy as np
from jax import lax

SH = 64
NR = 32
CAP = 4
TR = 512
LB = 128
P_SIZE = 4
RECOV = 768
NEB = 8
NEL = 1024
MBLK = 8
GCAP = 2
SLABS = 8
LATS = 4
RBLOCKS = 1024
EBLOCKS = 256
N_SLAB = 8


def panel_common(key):
    keys = jax.random.split(key, 3)
    magnitude = jax.random.uniform(keys[0], (SLABS, LATS, TR), jnp.float32, 0.75, 0.9)
    phase = jax.random.uniform(keys[1], (SLABS, LATS, TR), jnp.float32, -math.pi, math.pi)
    noise = jax.random.normal(keys[2], (SLABS, LATS, 2, TR, TR), jnp.float32) * (0.3 / math.sqrt(2.0 * TR))
    noise = jnp.clip(noise, -0.1, 0.1)
    diagonal = jnp.stack([magnitude * jnp.cos(phase), magnitude * jnp.sin(phase)], axis=2)
    identity = jnp.eye(TR, dtype=jnp.float32)
    return noise + identity * diagonal[..., :, None]


def draw_down_panel(key, part):
    return panel_common(jax.random.fold_in(key, 11))


def draw_up_panel(key, part):
    return panel_common(jax.random.fold_in(key, 12))


def touch_ends(result, rng, least, high):
    longest = result.shape.index(max(result.shape))
    spots = []
    for shift in (0, 1):
        where = [jax.random.randint(jax.random.fold_in(rng, axis), (), 0, length) for axis, length in enumerate(result.shape)]
        where[longest] = (where[longest] + shift) % result.shape[longest]
        spots.append(tuple(where))
    return result.at[spots[0]].set(least).at[spots[1]].set(high)


def shard_levels(key, extent, shards, least, high):
    gain, own = 1.0, jax.random.fold_in(key, 6)
    for position, blocks in shards:
        draws = jnp.exp(jax.random.uniform(jax.random.fold_in(own, position), (blocks,), jnp.float32, least / len(shards), high / len(shards)))
        gain = gain * jnp.repeat(draws, extent[position] // blocks).reshape([-1 if axis == position else 1 for axis in range(len(extent))])
    return gain


def routed_block(rng, own, number, rows, count, top, bound, skew):
    ranking = jax.random.permutation(rng, count)
    crowded, common = portions_of(count, rows * top, bound, skew, True), portions_of(count, rows * top, bound, skew, False)
    places = jnp.arange(count)

    def named(sizes, turn):
        used = int((sizes > 0).sum())
        fixed = max(1, used // 4)
        shifted = fixed + (places - fixed + turn * (used - fixed)) % max(1, count - fixed)
        return jnp.zeros((count,), jnp.int32).at[ranking[jnp.where(places < fixed, places, shifted)]].set(jnp.asarray(sizes, jnp.int32))

    sizes = jnp.where(number % 4 == 0, named(crowded, number // 4), named(common, number - number // 4 - 1))
    mixed = jax.random.permutation(jax.random.fold_in(own, 3), count)
    giver, receiver = mixed[0:count // 2 * 2:2], mixed[1:count // 2 * 2:2]
    slack = jnp.minimum(sizes[giver] - 1, bound - sizes[receiver]) // 2
    slack = jnp.where((giver == ranking[0]) | (receiver == ranking[0]) | (sizes[receiver] == 0), 0, jnp.maximum(slack, 0))
    shifted = jax.random.randint(jax.random.fold_in(own, 4), (count // 2,), 0, 1 << 20) % (slack + 1)
    sizes = sizes.at[giver].add(-shifted).at[receiver].add(shifted)
    items = jnp.searchsorted(jnp.cumsum(sizes), jnp.arange(rows * top), side="right").astype(jnp.int32)
    listing = items.reshape(top, rows).T
    listing = listing[jax.random.permutation(jax.random.fold_in(own, 1), rows)]
    turn = jax.random.randint(jax.random.fold_in(own, 2), (rows, 1), 0, top)
    return jnp.take_along_axis(listing, (jnp.arange(top)[None, :] + turn) % top, axis=1)


def portions_of(number_of, total, reach, slope, full):
    portions = [(1 << 20) // math.isqrt(standing ** slope) + 1 for standing in range(1, number_of + 1)]
    largest = reach if full else min(reach, max(-(-total // number_of), total * portions[0] // sum(portions)))
    least = 1 if total - largest >= number_of - 1 else 0
    given, rest = [largest] + [least] * (number_of - 1), total - largest - least * (number_of - 1)
    while rest > 0:
        free = [i for i in range(1, number_of) if given[i] < largest] or [i for i in range(1, number_of) if given[i] < reach]
        mass, left = sum([portions[i] for i in free]), rest
        for i in free:
            addition = min(reach - given[i], max(1, left * portions[i] // mass), rest)
            given[i] = given[i] + addition
            rest = rest - addition
    return np.array(given)


def scatter_about(stream_key, dims, spread, bound, shards=(), kind=jnp.bfloat16):
    array = spread * jax.random.normal(stream_key, dims, jnp.float32)
    if shards:
        array = array * shard_levels(stream_key, dims, shards, -0.22, 0.18)
    return jnp.clip(array, -bound, bound).astype(kind)


def setup_inputs(seed: int = 0) -> dict:
    splits = jax.random.split(jax.random.key(seed), 12)
    residual_blocks = scatter_about(splits[0], (RBLOCKS, 2, SH, LB), 0.25, 1.5, ((0, 32),), jnp.float32)
    residual_slab_keys = jax.random.split(jax.random.fold_in(splits[1], 1), RBLOCKS // NR)
    residual_slab_turns = jax.random.permutation(jax.random.fold_in(splits[1], 3), RBLOCKS // NR)
    residual_slab = jax.vmap(lambda own, number: routed_block(jax.random.fold_in(splits[1], 2), own, number, NR, N_SLAB, 1, CAP, 2))(residual_slab_keys, residual_slab_turns).reshape((RBLOCKS, 1))
    residual_pos = touch_ends(jax.random.randint(splits[2], (RBLOCKS,), 0, P_SIZE), jax.random.fold_in(splits[2], 1), 0, P_SIZE - 1).astype(jnp.int32)
    shot_ids = jax.random.permutation(splits[3], SH).astype(jnp.int32)
    wavelet = scatter_about(splits[4], (SH, 2), 1.0, 4.0, (), jnp.float32)
    down_panel = draw_down_panel(jax.random.fold_in(splits[11], 71), 0)
    up_panel = draw_up_panel(jax.random.fold_in(splits[11], 71), 0)
    recovery = scatter_about(splits[7], (SLABS, LATS, 2, RECOV, NEL), (4 * RECOV) ** -0.5, 0.109375, ((0, 8), (1, 4)), jnp.float32)
    forward_field = scatter_about(splits[8], (SLABS, LATS, 2, SH, NEL), 0.5, 3.0, ((0, 8), (1, 4)), jnp.float32)
    element_owner_keys = jax.random.split(jax.random.fold_in(splits[9], 1), EBLOCKS // NEB)
    element_owner_turns = jax.random.permutation(jax.random.fold_in(splits[9], 3), EBLOCKS // NEB)
    element_owner = jax.vmap(lambda own, number: routed_block(jax.random.fold_in(splits[9], 2), own, number, NEB, N_SLAB, 1, GCAP, 2))(element_owner_keys, element_owner_turns).reshape((EBLOCKS, 1))
    element_slot = touch_ends(jax.random.randint(splits[10], (EBLOCKS,), 0, MBLK), jax.random.fold_in(splits[10], 1), 0, MBLK - 1).astype(jnp.int32)
    return {"residual_blocks": residual_blocks, "residual_slab": residual_slab, "residual_pos": residual_pos, "shot_ids": shot_ids, "wavelet": wavelet, "down_panel": down_panel, "up_panel": up_panel, "recovery": recovery, "forward_field": forward_field, "element_owner": element_owner, "element_slot": element_slot}


def complex_product(vector, panel):
    value_re = vector[..., 0, :, :]
    value_im = vector[..., 1, :, :]
    panel_re = panel[..., 0, :, :]
    panel_im = panel[..., 1, :, :]
    first = jnp.matmul(value_re, panel_re, precision=lax.Precision.HIGHEST) - jnp.matmul(value_im, panel_im, precision=lax.Precision.HIGHEST)
    second = jnp.matmul(value_re, panel_im, precision=lax.Precision.HIGHEST) + jnp.matmul(value_im, panel_re, precision=lax.Precision.HIGHEST)
    return jnp.stack([first, second], axis=-3)


def reference(residual_blocks, residual_slab, residual_pos, shot_ids, wavelet, down_panel, up_panel, recovery, forward_field, element_owner, element_slot):
    block_rows = jnp.arange(RBLOCKS, dtype=jnp.int32)
    lateral = (block_rows // NR) % LATS
    target = ((residual_slab[:, 0] * LATS + lateral) * P_SIZE + residual_pos).astype(jnp.int32)
    summed = jax.ops.segment_sum(residual_blocks, target, num_segments=SLABS * LATS * P_SIZE)
    summed = summed.reshape(SLABS, LATS, P_SIZE, 2, SH, LB).transpose(0, 1, 3, 4, 2, 5).reshape(SLABS, LATS, 2, SH, TR)
    weights = wavelet[shot_ids]
    weight_re = weights[:, 0][:, None]
    weight_im = weights[:, 1][:, None]
    summed_re = summed[:, :, 0]
    summed_im = summed[:, :, 1]
    sources = jnp.stack([weight_re * summed_re - weight_im * summed_im, weight_re * summed_im + weight_im * summed_re], axis=2)

    def down_turn(carry, inputs):
        panel, source = inputs
        value = complex_product(carry, panel) + source
        return value, value

    start = jnp.zeros((LATS, 2, SH, TR), jnp.float32)
    unused, downs = lax.scan(down_turn, start, (down_panel, sources))

    def up_turn(carry, inputs):
        panel, source = inputs
        value = complex_product(carry, panel) + source
        return value, value

    unused, ups = lax.scan(up_turn, start, (up_panel, downs), reverse=True)
    left_rim = jnp.pad(ups[:, :-1, :, :, TR - LB:], ((0, 0), (1, 0), (0, 0), (0, 0), (0, 0)))
    right_rim = jnp.pad(ups[:, 1:, :, :, :LB], ((0, 0), (0, 1), (0, 0), (0, 0), (0, 0)))
    extended = jnp.concatenate([left_rim, ups, right_rim], axis=-1)
    interior = complex_product(extended, recovery)
    gradient = jnp.sum(forward_field * interior, axis=(2, 3)) * (SH ** -0.5)
    element_blocks = gradient.reshape(EBLOCKS, LB)
    element_rows = jnp.arange(EBLOCKS, dtype=jnp.int32)
    element_lat = (element_rows // NEB) % LATS
    element_target = ((element_owner[:, 0] * LATS + element_lat) * MBLK + element_slot).astype(jnp.int32)
    model = jax.ops.segment_sum(element_blocks, element_target, num_segments=SLABS * LATS * MBLK)
    return ups, model.reshape(SLABS, LATS, MBLK, LB)
```

```python
import functools

import jax
import jax.numpy as jnp
from jax import lax
from jax.experimental import pallas as pl
from jax.experimental.pallas import tpu as pltpu
from jax.sharding import PartitionSpec as P

MBLK = 8
VMEM = pl.BlockSpec(memory_space=pltpu.VMEM)
SMEM = pl.BlockSpec(memory_space=pltpu.SMEM)
ANY = pl.BlockSpec(memory_space=pl.ANY)
LIMIT = 40 * 1024 * 1024


def split(value):
    high = value.astype(jnp.bfloat16)
    low = (value - high.astype(jnp.float32)).astype(jnp.bfloat16)
    return high, low


def product(vector, high, low):
    m, n = vector.shape[1], high.shape[1] // 2
    top, rest = split(vector.reshape(2 * m, -1))
    wide = jnp.dot(top, high, preferred_element_type=jnp.float32)
    wide += jnp.dot(rest, high, preferred_element_type=jnp.float32)
    wide += jnp.dot(top, low, preferred_element_type=jnp.float32)
    return wide[:m, :n] - wide[m:, n:], wide[:m, n:] + wide[m:, :n]


def halves_kernel(panel_ref, high_ref, low_ref):
    n = panel_ref.shape[-1]
    for part in range(2):
        high, low = split(panel_ref[part])
        high_ref[:, part * n : (part + 1) * n] = high
        low_ref[:, part * n : (part + 1) * n] = low


def halves(panel, rows=128):
    _, k, n = panel.shape
    block = pl.BlockSpec((rows, 2 * n), lambda i: (i, 0))
    return pl.pallas_call(
        halves_kernel,
        grid=(k // rows,),
        in_specs=[pl.BlockSpec((2, rows, n), lambda i: (0, i, 0))],
        out_specs=[block, block],
        out_shape=[jax.ShapeDtypeStruct((k, 2 * n), jnp.bfloat16)] * 2,
        compiler_params=pltpu.CompilerParams(vmem_limit_bytes=LIMIT),
        name="halves",
    )(panel)


def collect_kernel(group_ref, slab_ref, pos_ref, blocks_ref, *outs):
    groups = len(outs)
    width = blocks_ref.shape[-1]
    for out in outs:
        out[...] = jnp.zeros_like(out)

    def place(row, carry):
        slab = slab_ref[row, 0]
        group = lax.rem(lax.div(slab, 2) - group_ref[0] + groups, groups)
        side = lax.rem(slab, 2)
        lanes = pl.ds(pl.multiple_of(pos_ref[row] * width, width), width)
        for number, out in enumerate(outs):

            @pl.when(group == number)
            def _():
                for part in range(2):
                    out[side, part, :, lanes] += blocks_ref[row, part]

        return carry

    lax.fori_loop(0, blocks_ref.shape[0], place, 0)


def collect(group, slab, pos, blocks, groups, trace):
    _, _, shots, _ = blocks.shape
    return pl.pallas_call(
        collect_kernel,
        in_specs=[SMEM, SMEM, SMEM, VMEM],
        out_specs=[VMEM] * groups,
        out_shape=[jax.ShapeDtypeStruct((2, 2, shots, trace), jnp.float32)] * groups,
        compiler_params=pltpu.CompilerParams(vmem_limit_bytes=LIMIT),
        name="collect",
    )(group, slab, pos, blocks)


def pair_kernel(odd_ref, arrived_ref, dh_ref, dl_ref, uh_ref, ul_ref, high_ref, low_ref):
    n = high_ref.shape[-1] // 2

    def run(high, low):
        for part, value in enumerate(product(arrived_ref[...], high[...], low[...])):
            top, rest = split(value)
            high_ref[:, part * n : (part + 1) * n] = top
            low_ref[:, part * n : (part + 1) * n] = rest

    @pl.when(odd_ref[0] == 1)
    def _():
        run(dh_ref, dl_ref)

    @pl.when(odd_ref[0] == 0)
    def _():
        run(uh_ref, ul_ref)


def pair_panel(odd, arrived, down, up, rows=128):
    _, k, n = arrived.shape
    whole = pl.BlockSpec((k, 2 * n), lambda i: (0, 0))
    block = pl.BlockSpec((rows, 2 * n), lambda i: (i, 0))
    return pl.pallas_call(
        pair_kernel,
        grid=(k // rows,),
        in_specs=[SMEM, pl.BlockSpec((2, rows, n), lambda i: (0, i, 0))] + [whole] * 4,
        out_specs=[block, block],
        out_shape=[jax.ShapeDtypeStruct((k, 2 * n), jnp.bfloat16)] * 2,
        compiler_params=pltpu.CompilerParams(vmem_limit_bytes=LIMIT),
        name="pair_panel",
    )(odd, arrived, *down, *up)


def step_kernel(active_ref, arrived_ref, high_ref, low_ref, own_ref, old_ref, out_ref):
    @pl.when(active_ref[0] == 1)
    def _():
        real, imag = product(arrived_ref[...], high_ref[...], low_ref[...])
        out_ref[0] = real + own_ref[0]
        out_ref[1] = imag + own_ref[1]

    @pl.when(active_ref[0] == 0)
    def _():
        out_ref[...] = old_ref[...]


def step(active, arrived, panel, own, old):
    return pl.pallas_call(
        step_kernel,
        in_specs=[SMEM] + [VMEM] * 5,
        out_specs=VMEM,
        out_shape=jax.ShapeDtypeStruct(own.shape, jnp.float32),
        compiler_params=pltpu.CompilerParams(vmem_limit_bytes=LIMIT),
        name="step",
    )(active, arrived, *panel, own, old)


def middle_kernel(field_ref, high_ref, low_ref, out_ref):
    real, imag = product(field_ref[...], high_ref[...], low_ref[...])
    out_ref[0] = real
    out_ref[1] = imag


def middle(field, high, low, width):
    _, shots, trace = field.shape
    n = high.shape[-1] // 2
    return pl.pallas_call(
        middle_kernel,
        in_specs=[VMEM] * 3,
        out_specs=VMEM,
        out_shape=jax.ShapeDtypeStruct((2, shots, n), jnp.float32),
        compiler_params=pltpu.CompilerParams(vmem_limit_bytes=LIMIT),
        name="middle",
    )(field, high[width : width + trace], low[width : width + trace])


def rim_kernel(owner_ref, slot_ref, part_ref, left_ref, right_ref, *refs):
    lh_ref, ll_ref, rh_ref, rl_ref, forward_ref, out_ref = refs
    shots, width = left_ref.shape[1], left_ref.shape[2]
    real, imag = product(left_ref[...], lh_ref[...], ll_ref[...])
    more_real, more_imag = product(right_ref[...], rh_ref[...], rl_ref[...])
    total = forward_ref[0] * (part_ref[0] + real + more_real)
    total += forward_ref[1] * (part_ref[1] + imag + more_imag)
    gradient = jnp.sum(total, axis=0, keepdims=True) * shots ** (-0.5)
    out_ref[...] = jnp.zeros_like(out_ref)
    for block in range(gradient.shape[1] // width):
        row = owner_ref[block, 0] * MBLK + slot_ref[block]
        out_ref[pl.ds(row, 1), :] += gradient[:, block * width : (block + 1) * width]


def rim(owner, slot, part, left, right, high, low, forward, slabs):
    width = left.shape[2]
    return pl.pallas_call(
        rim_kernel,
        in_specs=[SMEM, SMEM] + [VMEM] * 8,
        out_specs=VMEM,
        out_shape=jax.ShapeDtypeStruct((slabs * MBLK, width), jnp.float32),
        compiler_params=pltpu.CompilerParams(vmem_limit_bytes=LIMIT),
        name="rim",
    )(owner, slot, part, left, right, high[:width], low[:width], high[-width:], low[-width:], forward)


def body(
    residual_blocks,
    residual_slab,
    residual_pos,
    shot_ids,
    wavelet,
    down_panel,
    up_panel,
    recovery,
    forward_field,
    element_owner,
    element_slot,
):
    slabs = lax.axis_size("slab")
    lats = lax.axis_size("lat")
    groups = slabs // 2
    shots, width = residual_blocks.shape[2:]
    trace = down_panel.shape[-1]
    me = lax.axis_index("slab").astype(jnp.int32)
    group, odd = me // 2, me % 2
    is_odd = odd == 1

    def flag(condition):
        return condition.astype(jnp.int32).reshape(1)

    def hop(value, route):
        return lax.ppermute(value, "slab", route)

    parts = collect(
        group.reshape(1), residual_slab, residual_pos, residual_blocks, groups, trace
    )
    summed = parts[0]
    for turn in range(1, groups):
        summed = summed + hop(parts[turn], [(s, (s + 2 * turn) % slabs) for s in range(slabs)])

    panel_out = jnp.where(is_odd, up_panel[0, 0], down_panel[0, 0])
    panel_in = hop(panel_out, [(s, s ^ 1) for s in range(slabs)])
    down = halves(down_panel[0, 0])
    up = halves(up_panel[0, 0])
    maps = halves(recovery[0, 0])
    pair = pair_panel(odd.reshape(1), panel_in, down, up)

    picker = shot_ids[:, None] == jnp.arange(shots, dtype=jnp.int32)[None, :]
    weights = jnp.sum(jnp.where(picker[:, :, None], wavelet[None], 0.0), axis=1)
    weight_re, weight_im = weights[:, 0:1], weights[:, 1:2]

    def weighted(value):
        return jnp.stack(
            [
                weight_re * value[0] - weight_im * value[1],
                weight_re * value[1] + weight_im * value[0],
            ]
        )

    source_even = weighted(summed[0] + hop(summed[0], [(s, s ^ 1) for s in range(slabs)]))
    source_odd = weighted(summed[1] + hop(summed[1], [(s, s + 1) for s in range(0, slabs, 2)]))

    own = step(flag(is_odd), source_even, down, source_odd, source_odd)
    state = own
    for k in range(1, groups):
        arrived = hop(state, [(2 * k - 1, 2 * k + 1)])
        state = step(flag(me == 2 * k + 1), arrived, pair, own, state)
    before = hop(state, [(2 * k - 1, 2 * k) for k in range(1, groups)])
    beside = hop(state, [(2 * k + 1, 2 * k) for k in range(groups)])
    even_down = step(flag(~is_odd), before, down, source_even, source_even)
    own = step(flag(~is_odd), beside, up, even_down, even_down)
    above = own
    for k in range(groups - 2, -1, -1):
        arrived = hop(above, [(2 * k + 2, 2 * k)])
        above = step(flag(me == 2 * k), arrived, pair, own, above)
    after = hop(above, [(2 * k + 2, 2 * k + 1) for k in range(groups - 1)])
    ups = step(flag(is_odd), after, up, state, above)

    left = lax.ppermute(ups[:, :, trace - width :], "lat", [(i, i + 1) for i in range(lats - 1)])
    right = lax.ppermute(ups[:, :, :width], "lat", [(i + 1, i) for i in range(lats - 1)])
    part = middle(ups, *maps, width)
    outgoing = rim(
        element_owner, element_slot, part, left, right, *maps, forward_field[0, 0], slabs
    )
    arrived = lax.all_to_all(outgoing, "slab", split_axis=0, concat_axis=0, tiled=True)
    model = jnp.sum(arrived.reshape(slabs, MBLK, width), axis=0)
    return (ups[None, None], model[None, None])


def solution(mesh):
    placed = (
        P(("slab", "lat"), None, None, None),
        P(("slab", "lat"), None),
        P(("slab", "lat")),
        P(),
        P(),
        P("slab", "lat", None, None, None),
        P("slab", "lat", None, None, None),
        P("slab", "lat", None, None, None),
        P("slab", "lat", None, None, None),
        P(("slab", "lat"), None),
        P(("slab", "lat")),
    )
    return jax.shard_map(
        body,
        mesh=mesh,
        in_specs=placed,
        out_specs=(P("slab", "lat", None, None, None), P("slab", "lat", None, None)),
        check_vma=False,
    )
```

```python
import jax
import jax.numpy as jnp
from jax import lax
from jax.experimental import pallas as pl
from jax.experimental.pallas import tpu as pltpu
from jax.sharding import PartitionSpec as P

MBLK = 8
VMEM = pl.BlockSpec(memory_space=pltpu.VMEM)
SMEM = pl.BlockSpec(memory_space=pltpu.SMEM)
ANY = pl.BlockSpec(memory_space=pl.ANY)
PARAMS = pltpu.CompilerParams(vmem_limit_bytes=16 * 1024 * 1024)


def floats(*shape):
    return jax.ShapeDtypeStruct(shape, jnp.float32)


def cost(flops):
    return pl.CostEstimate(flops=flops, bytes_accessed=flops // 1000, transcendentals=0)


def split(value):
    high = value.astype(jnp.bfloat16)
    low = (value - high.astype(jnp.float32)).astype(jnp.bfloat16)
    return high, low


def product(vector, high, low):
    m, n = vector.shape[1], high.shape[1] // 2
    top, rest = split(vector.reshape(2 * m, -1))
    wide = jnp.dot(top, high, preferred_element_type=jnp.float32)
    wide += jnp.dot(rest, high, preferred_element_type=jnp.float32)
    wide += jnp.dot(top, low, preferred_element_type=jnp.float32)
    return wide[:m, :n] - wide[m:, n:], wide[:m, n:] + wide[m:, :n]


def call(kernel, name, ins, outs, out_specs, after, flops=0, **keywords):
    specs, values = zip(*ins)
    count = len(values)

    def run(*refs):
        kernel(*refs[:count], *refs[count + len(after) :])

    return pl.pallas_call(
        run,
        in_specs=list(specs) + [ANY] * len(after),
        out_specs=out_specs,
        out_shape=outs,
        compiler_params=PARAMS,
        cost_estimate=cost(flops) if flops else None,
        name=name,
        **keywords,
    )(*values, *after)


def halves_kernel(panel_ref, high_ref, low_ref):
    n = panel_ref.shape[-1]
    for part in range(2):
        high, low = split(panel_ref[part])
        high_ref[:, part * n : (part + 1) * n] = high
        low_ref[:, part * n : (part + 1) * n] = low


def halves(panel, after, rows=128):
    _, k, n = panel.shape
    block = pl.BlockSpec((rows, 2 * n), lambda i: (i, 0))
    return call(
        halves_kernel,
        "halves",
        [(pl.BlockSpec((2, rows, n), lambda i: (0, i, 0)), panel)],
        [jax.ShapeDtypeStruct((k, 2 * n), jnp.bfloat16)] * 2,
        [block, block],
        after,
        2 * 10**9,
        grid=(k // rows,),
    )


def hold_kernel(panel_ref, out_ref):
    out_ref[...] = panel_ref[...]


def hold(panel, after, rows=128):
    _, k, n = panel.shape
    block = pl.BlockSpec((2, rows, n), lambda i: (0, i, 0))
    return call(
        hold_kernel, "hold", [(block, panel)], floats(2, k, n), block, after, grid=(k // rows,)
    )


def collect_kernel(me_ref, slab_ref, pos_ref, blocks_ref, *outs, sets):
    width = blocks_ref.shape[-1]
    me = me_ref[0]
    for out in outs:
        out[...] = jnp.zeros_like(out)

    def place(row, carry):
        slab = slab_ref[row]
        apart = lax.bitwise_xor(slab, me)
        side = lax.rem(apart, 2)
        lanes = pl.ds(pl.multiple_of(pos_ref[row] * width, width), width)
        for number, (size, which) in enumerate(sets):
            turn = lax.rem(lax.div(apart, 2), 2) if size == 4 else 0
            for other in range(2):

                @pl.when((lax.div(slab, size) == which) & (side == other))
                def _():
                    for part in range(2):
                        outs[2 * number + other][turn, part, :, lanes] += blocks_ref[row, part]

        return carry

    lax.fori_loop(0, blocks_ref.shape[0], place, 0)


def collect(me, slab, pos, blocks, sets, trace, after):
    shots = blocks.shape[2]
    shapes = [floats(size // 2, 2, shots, trace) for size, _ in sets for _ in range(2)]
    outs = call(
        lambda *refs: collect_kernel(*refs, sets=sets),
        "collect",
        [(SMEM, me), (SMEM, slab), (SMEM, pos), (VMEM, blocks)],
        shapes,
        [VMEM] * len(shapes),
        after,
        2 * 10**9,
    )
    return [outs[2 * i : 2 * i + 2] for i in range(len(sets))]


def ready_kernel(ids_ref, owner_ref, slot_ref, wavelet_ref, weights_ref, rows_ref):
    def pick(row, carry):
        weights_ref[pl.ds(row, 1), :] = wavelet_ref[pl.ds(ids_ref[row], 1), :]
        return carry

    lax.fori_loop(0, weights_ref.shape[0], pick, 0)

    def target(row, carry):
        rows_ref[row] = owner_ref[row] * MBLK + slot_ref[row]
        return carry

    lax.fori_loop(0, rows_ref.shape[0], target, 0)


def ready(ids, owner, slot, wavelet, after):
    return call(
        ready_kernel,
        "ready",
        [(SMEM, ids), (SMEM, owner), (SMEM, slot), (VMEM, wavelet)],
        [floats(*wavelet.shape), jax.ShapeDtypeStruct(slot.shape, jnp.int32)],
        [VMEM, SMEM],
        after,
    )


def join_kernel(mine_ref, arrived_ref, *refs, count):
    outs = refs[len(refs) - count :]
    last = mine_ref.shape[0] - 1
    outs[0][...] = mine_ref[0] + arrived_ref[0]
    outs[1][...] = mine_ref[last] + arrived_ref[last]
    if count == 3:
        outs[2][...] = refs[0][...]


def join(mine, arrived, following, after):
    count = 2 + len(following)
    return call(
        lambda *refs: join_kernel(*refs, count=count),
        "join",
        [(VMEM, value) for value in (mine, arrived, *following)],
        [floats(*mine.shape[1:])] * 2 + [floats(*value.shape) for value in following],
        [VMEM] * count,
        after,
    )


def add_kernel(one_ref, two_ref, out_ref):
    out_ref[...] = one_ref[...] + two_ref[...]


def add(one, two, after):
    return call(add_kernel, "add", [(VMEM, one), (VMEM, two)], floats(*one.shape), VMEM, after)


def source_kernel(one_ref, two_ref, weights_ref, out_ref):
    weight_re, weight_im = weights_ref[:, 0:1], weights_ref[:, 1:2]
    real, imag = one_ref[0] + two_ref[0], one_ref[1] + two_ref[1]
    out_ref[0] = weight_re * real - weight_im * imag
    out_ref[1] = weight_re * imag + weight_im * real


def source(one, two, weights, after):
    return call(
        source_kernel,
        "source",
        [(VMEM, one), (VMEM, two), (VMEM, weights)],
        floats(*one.shape),
        VMEM,
        after,
    )


def cleave_kernel(field_ref, *outs):
    rows = outs[0].shape[1]
    for number, out in enumerate(outs):
        out[...] = field_ref[:, number * rows : (number + 1) * rows]


def cleave(field, streams, after):
    parts, shots, trace = field.shape
    return call(
        cleave_kernel,
        "cleave",
        [(VMEM, field)],
        [floats(parts, shots // streams, trace)] * streams,
        [VMEM] * streams,
        after,
    )


def down_kernel(me_ref, arrived_ref, high_ref, low_ref, own_ref, old_ref, out_ref, *, at, cut):
    @pl.when(me_ref[0] == at)
    def _():
        real, imag = product(arrived_ref[...], high_ref[...], low_ref[...])
        out_ref[0] = real + own_ref[0, cut]
        out_ref[1] = imag + own_ref[1, cut]

    @pl.when(me_ref[0] != at)
    def _():
        out_ref[...] = old_ref[...]


def down_step(me, at, arrived, panel, own, first, old, after):
    cut = slice(first, first + old.shape[1])
    return call(
        lambda *refs: down_kernel(*refs, at=at, cut=cut),
        "down",
        [(SMEM, me)] + [(VMEM, value) for value in (arrived, *panel, own, old)],
        floats(*old.shape),
        VMEM,
        after,
    )


def up_kernel(me_ref, arrived_ref, oh, ol, beside_ref, eh, el, own_ref, old_ref, out_ref, *, at, top):
    @pl.when(me_ref[0] == at)
    def _():
        if top:
            out_ref[...] = beside_ref[...]
        else:
            real, imag = product(arrived_ref[...], oh[...], ol[...])
            out_ref[0] = real + beside_ref[0]
            out_ref[1] = imag + beside_ref[1]
        real, imag = product(out_ref[...], eh[...], el[...])
        out_ref[0] = real + own_ref[0]
        out_ref[1] = imag + own_ref[1]

    @pl.when(me_ref[0] != at)
    def _():
        out_ref[...] = old_ref[...]


def up_step(me, at, arrived, odd, beside, even, own, old, top, after):
    return call(
        lambda *refs: up_kernel(*refs, at=at, top=top),
        "up",
        [(SMEM, me)] + [(VMEM, value) for value in (arrived, *odd, beside, *even, own, old)],
        floats(*own.shape),
        VMEM,
        after,
    )


def finish_kernel(me_ref, *refs, streams, width):
    arrived, owns, olds = (refs[i * streams : (i + 1) * streams] for i in range(3))
    high_ref, low_ref, out_ref, head_ref, tail_ref = refs[3 * streams :]
    trace = out_ref.shape[-1]

    @pl.when(lax.rem(me_ref[0], 2) == 1)
    def _():
        field = jnp.concatenate([ref[...] for ref in arrived], axis=1)
        real, imag = product(field, high_ref[...], low_ref[...])
        out_ref[0] = real + jnp.concatenate([ref[0] for ref in owns], axis=0)
        out_ref[1] = imag + jnp.concatenate([ref[1] for ref in owns], axis=0)

    @pl.when(lax.rem(me_ref[0], 2) == 0)
    def _():
        out_ref[...] = jnp.concatenate([ref[...] for ref in olds], axis=1)

    head_ref[...] = out_ref[:, :, :width]
    tail_ref[...] = out_ref[:, :, trace - width :]


def finish(me, arrived, panel, own, old, width, after):
    streams = len(own)
    _, rows, trace = own[0].shape
    shots = rows * streams
    return call(
        lambda *refs: finish_kernel(*refs, streams=streams, width=width),
        "finish",
        [(SMEM, me)] + [(VMEM, value) for value in (*arrived, *own, *old, *panel)],
        [floats(2, shots, trace), floats(2, shots, width), floats(2, shots, width)],
        [VMEM] * 3,
        after,
    )


def middle_kernel(field_ref, high_ref, low_ref, forward_ref, out_ref, *, width):
    inner = slice(width, width + field_ref.shape[-1])
    real, imag = product(field_ref[...], high_ref[inner], low_ref[inner])
    total = forward_ref[0] * real + forward_ref[1] * imag
    out_ref[...] = jnp.sum(total, axis=0, keepdims=True)


def middle(field, maps, forward, width):
    return call(
        lambda *refs: middle_kernel(*refs, width=width),
        "middle",
        [(VMEM, value) for value in (field, *maps, forward)],
        floats(1, forward.shape[-1]),
        VMEM,
        (),
        4 * 10**9,
    )


def rim_kernel(rows_ref, part_ref, left_ref, right_ref, high_ref, low_ref, forward_ref, out_ref):
    shots, width = left_ref.shape[1], left_ref.shape[2]
    depth = high_ref.shape[0]

    def ends(ref):
        return jnp.concatenate([ref[:width], ref[depth - width :]], axis=0)

    field = jnp.concatenate([left_ref[...], right_ref[...]], axis=-1)
    real, imag = product(field, ends(high_ref), ends(low_ref))
    total = forward_ref[0] * real + forward_ref[1] * imag
    gradient = part_ref[...] + jnp.sum(total, axis=0, keepdims=True)
    gradient = gradient * shots ** (-0.5)
    out_ref[...] = jnp.zeros_like(out_ref)
    for block in range(gradient.shape[1] // width):
        row = rows_ref[block]
        out_ref[pl.ds(row, 1), :] += gradient[:, block * width : (block + 1) * width]


def rim(rows, part, left, right, maps, forward, slabs):
    return call(
        rim_kernel,
        "rim",
        [(SMEM, rows)] + [(VMEM, value) for value in (part, left, right, *maps, forward)],
        floats(slabs * MBLK, left.shape[2]),
        VMEM,
        (),
    )


def body(
    residual_blocks,
    residual_slab,
    residual_pos,
    shot_ids,
    wavelet,
    down_panel,
    up_panel,
    recovery,
    forward_field,
    element_owner,
    element_slot,
):
    slabs = lax.axis_size("slab")
    lats = lax.axis_size("lat")
    groups = slabs // 2
    shots, width = residual_blocks.shape[2:]
    trace = down_panel.shape[-1]
    streams = 2 if shots % 32 == 0 else 1
    lanes = range(streams)
    rows = shots // streams
    me = lax.axis_index("slab").astype(jnp.int32).reshape(1)
    quads = slabs // 4
    sets = [(2, 0), (2, 1)] + [(4, quad) for quad in range(1, quads)]
    hops = quads.bit_length() - 1
    swapping = [(s, s ^ 1) for s in range(slabs)]

    def hop(value, route):
        return lax.ppermute(value, "slab", route)

    def toward(number, turn):
        size, which = sets[number]
        if size == 4 and turn == 0:
            return [(s, s ^ 2) for s in range(slabs)]
        bit = 1 << (turn if size == 2 else turn - 1)
        return [
            (s, s ^ (size * bit)) for s in range(slabs) if ((s // size) ^ which) & (2 * bit - 1) == bit
        ]

    def gather(which, after):
        return collect(
            me, residual_slab[:, 0], residual_pos, residual_blocks, which, trace, after
        )

    parts = gather(sets[:1], [])
    swapped = [hop(parts[0][1], swapping)]
    weights, targets = ready(shot_ids, element_owner[:, 0], element_slot, wavelet, [parts[0][0]])
    down = halves(down_panel[0, 0], [weights])
    parts += gather(sets[1:], [down[0]])
    total, sent, base = {}, {}, {}

    def stage_join(number, token):
        following = [part[1] for part in parts[number + 1 : number + 2]]
        keep, joined, *gate = join(parts[number][0], swapped[number], following, token)
        total[number] = keep
        sent[number] = hop(joined, toward(number, 0))
        swapped.extend(hop(value, swapping) for value in gate)
        return [keep]

    def stage_add(number, turn, token):
        total[number] = add(total[number], sent[number], token)
        sent[number] = hop(total[number], toward(number, turn))
        return [total[number]]

    def stage_source(number, token):
        base[number] = source(total[number], sent[number], weights, token)
        return [base[number]]

    token = stage_join(0, [parts[1][0]])
    for turn in range(1, hops + 1):
        token = stage_add(0, turn, token)
    token = stage_join(1, token)
    up = halves(up_panel[0, 0], token)
    maps = halves(recovery[0, 0], [up[0]])
    token = stage_add(1, 1, [maps[0]])
    token = stage_source(0, token)
    state = list(cleave(base[0], streams, token))
    token = [state[0]]
    beside_panel = None
    for s in range(1, slabs):
        arrived = [hop(state[t], [(s - 1, s)]) for t in lanes]
        number = s // 2 if s < 4 else s // 4 + 1
        for t in lanes:
            state[t] = down_step(
                me, s, arrived[t], down, base[number], t * rows, state[t], token
            )
            token = [state[t]]
        if s == 1:
            for turn in range(2, hops + 1):
                token = stage_add(1, turn, token)
            token = stage_source(1, token)
        number = s // 4 + 2
        if number < len(sets):
            if s % 4 == 1:
                token = stage_join(number, token)
            if s % 4 == 2:
                for turn in range(1, hops + 1):
                    token = stage_add(number, turn, token)
            if s % 4 == 3:
                token = stage_source(number, token)
        if s == 1:
            held = hold(up_panel[0, 0], token)
            token = [held]
            beside_panel = hop(held, [(p + 1, p) for p in range(0, slabs - 2, 2)])
    beside = [hop(state[t], [(p + 1, p) for p in range(0, slabs, 2)]) for t in lanes]
    odd_up = halves(beside_panel, token)
    token = [odd_up[0]]
    above = list(state)
    for t in lanes:
        above[t] = up_step(
            me, slabs - 2, state[t], odd_up, beside[t], up, state[t], above[t], True, token
        )
        token = [above[t]]
    for p in range(slabs - 4, -1, -2):
        arrived = [hop(above[t], [(p + 2, p)]) for t in lanes]
        if p == 0:
            after = [hop(above[t], [(q + 2, q + 1) for q in range(0, slabs - 2, 2)]) for t in lanes]
        for t in lanes:
            above[t] = up_step(
                me, p, arrived[t], odd_up, beside[t], up, state[t], above[t], False, token
            )
            token = [above[t]]
    ups, head, tail = finish(me, after, up, state, above, width, token)

    left = lax.ppermute(tail, "lat", [(i, i + 1) for i in range(lats - 1)])
    right = lax.ppermute(head, "lat", [(i + 1, i) for i in range(lats - 1)])
    part = middle(ups, maps, forward_field[0, 0], width)
    outgoing = rim(targets, part, left, right, maps, forward_field[0, 0], slabs)
    arrived = lax.all_to_all(outgoing, "slab", split_axis=0, concat_axis=0, tiled=True)
    model = jnp.sum(arrived.reshape(slabs, MBLK, width), axis=0)
    return (ups[None, None], model[None, None])


def solution(mesh):
    placed = (
        P(("slab", "lat"), None, None, None),
        P(("slab", "lat"), None),
        P(("slab", "lat")),
        P(),
        P(),
        P("slab", "lat", None, None, None),
        P("slab", "lat", None, None, None),
        P("slab", "lat", None, None, None),
        P("slab", "lat", None, None, None),
        P(("slab", "lat"), None),
        P(("slab", "lat")),
    )
    return jax.shard_map(
        body,
        mesh=mesh,
        in_specs=placed,
        out_specs=(P("slab", "lat", None, None, None), P("slab", "lat", None, None)),
        check_vma=False,
    )
```

```python
import jax
import jax.numpy as jnp
from jax import lax
from jax.experimental import pallas as pl
from jax.experimental.pallas import tpu as pltpu
from jax.sharding import PartitionSpec as P

MBLK = 8
VMEM = pl.BlockSpec(memory_space=pltpu.VMEM)
SMEM = pl.BlockSpec(memory_space=pltpu.SMEM)
ANY = pl.BlockSpec(memory_space=pl.ANY)
HBM = pl.BlockSpec(memory_space=pltpu.HBM)
CHUNKS = 4


def floats(*shape):
    return jax.ShapeDtypeStruct(shape, jnp.float32)


def cost(flops):
    return pl.CostEstimate(flops=flops, bytes_accessed=flops // 1000, transcendentals=0)


def split(value):
    high = value.astype(jnp.bfloat16)
    low = (value - high.astype(jnp.float32)).astype(jnp.bfloat16)
    return high, low


def product(vector, high, low):
    m, n = vector.shape[1], high.shape[1] // 2
    top, rest = split(vector.reshape(2 * m, -1))
    wide = jnp.dot(top, high, preferred_element_type=jnp.float32)
    wide += jnp.dot(rest, high, preferred_element_type=jnp.float32)
    wide += jnp.dot(top, low, preferred_element_type=jnp.float32)
    return wide[:m, :n] - wide[m:, n:], wide[:m, n:] + wide[m:, :n]


def call(kernel, name, ins, outs, out_specs, after, flops=0, room=16, **keywords):
    specs, values = zip(*ins)
    count = len(values)

    def run(*refs):
        kernel(*refs[:count], *refs[count + len(after) :])

    return pl.pallas_call(
        run,
        in_specs=list(specs) + [ANY] * len(after),
        out_specs=out_specs,
        out_shape=outs,
        compiler_params=pltpu.CompilerParams(vmem_limit_bytes=room * 1024 * 1024),
        cost_estimate=cost(flops) if flops else None,
        name=name,
        **keywords,
    )(*values, *after)


def halves_kernel(panel_ref, high_ref, low_ref):
    n = panel_ref.shape[-1]
    for part in range(2):
        high, low = split(panel_ref[part])
        high_ref[:, part * n : (part + 1) * n] = high
        low_ref[:, part * n : (part + 1) * n] = low


def halves(panel, after, rows=128):
    _, k, n = panel.shape
    block = pl.BlockSpec((rows, 2 * n), lambda i: (i, 0))
    return call(
        halves_kernel,
        "halves",
        [(pl.BlockSpec((2, rows, n), lambda i: (0, i, 0)), panel)],
        [jax.ShapeDtypeStruct((k, 2 * n), jnp.bfloat16)] * 2,
        [block, block],
        after,
        2 * 10**9,
        grid=(k // rows,),
    )


def pair_kernel(me_ref, one_ref, two_ref, eh, el, high_ref, low_ref, *, top):
    k, n = one_ref.shape[1:]
    rows = 128
    place = lax.rem(me_ref[0], 4)

    def run(panel_ref):
        def chunk(i, carry):
            some = pl.ds(pl.multiple_of(i * rows, rows), rows)
            for part, value in enumerate(product(panel_ref[:, some], eh[...], el[...])):
                high, low = split(value)
                high_ref[some, part * n : (part + 1) * n] = high
                low_ref[some, part * n : (part + 1) * n] = low
            return carry

        lax.fori_loop(0, k // rows, chunk, 0)

    @pl.when((place == 0) & (me_ref[0] < top))
    def _():
        run(one_ref)

    @pl.when((place == 2) & (me_ref[0] < top))
    def _():
        run(two_ref)


def pair_panel(me, one, two, even, after, top):
    shape = jax.ShapeDtypeStruct(even[0].shape, jnp.bfloat16)
    return call(
        lambda *refs: pair_kernel(*refs, top=top),
        "pair",
        [(SMEM, me)] + [(VMEM, value) for value in (one, two, *even)],
        [shape, shape],
        [VMEM] * 2,
        after,
    )


def hold_kernel(me_ref, panel_ref, out_ref, *, place):
    @pl.when(lax.rem(me_ref[0], 4) == place)
    def _():
        out_ref[...] = panel_ref[...]


def hold(me, place, panel, after):
    return call(
        lambda *refs: hold_kernel(*refs, place=place),
        "hold",
        [(SMEM, me), (VMEM, panel)],
        floats(*panel.shape),
        VMEM,
        after,
    )


def collect_kernel(me_ref, slab_hbm, pos_hbm, blocks_hbm, *refs, sets):
    outs, (slab_ref, pos_ref, blocks_ref, sems) = refs[:-4], refs[-4:]
    count, width = blocks_ref.shape[0], blocks_ref.shape[-1]
    chunk = count // CHUNKS
    me = me_ref[0]
    copies = [
        pltpu.make_async_copy(slab_hbm, slab_ref, sems.at[CHUNKS]),
        pltpu.make_async_copy(pos_hbm, pos_ref, sems.at[CHUNKS + 1]),
    ]
    for i in range(CHUNKS):
        some = pl.ds(i * chunk, chunk)
        copies.append(pltpu.make_async_copy(blocks_hbm.at[some], blocks_ref.at[some], sems.at[i]))
    for copy in copies:
        copy.start()
    for out in outs:
        out[...] = jnp.zeros_like(out)
    copies[0].wait()
    copies[1].wait()

    def place(row, carry):
        slab = slab_ref[row]
        apart = lax.bitwise_xor(slab, me)
        side = lax.rem(apart, 2)
        lanes = pl.ds(pl.multiple_of(pos_ref[row] * width, width), width)
        for number, (size, which) in enumerate(sets):
            turn = lax.rem(lax.div(apart, 2), 2) if size == 4 else 0
            for other in range(2):

                @pl.when((lax.div(slab, size) == which) & (side == other))
                def _():
                    for part in range(2):
                        outs[2 * number + other][turn, part, :, lanes] += blocks_ref[row, part]

        return carry

    for i in range(CHUNKS):
        copies[2 + i].wait()
        lax.fori_loop(i * chunk, (i + 1) * chunk, place, 0)


def collect(me, slab, pos, blocks, sets, trace, after):
    shots = blocks.shape[2]
    shapes = [floats(size // 2, 2, shots, trace) for size, _ in sets for _ in range(2)]
    outs = call(
        lambda *refs: collect_kernel(*refs, sets=sets),
        "collect",
        [(SMEM, me), (HBM, slab), (HBM, pos), (HBM, blocks)],
        shapes,
        [VMEM] * len(shapes),
        after,
        2 * 10**9,
        59 if not after else 16,
        scratch_shapes=[
            pltpu.SMEM(slab.shape, jnp.int32),
            pltpu.SMEM(pos.shape, jnp.int32),
            pltpu.VMEM(blocks.shape, jnp.float32),
            pltpu.SemaphoreType.DMA((CHUNKS + 2,)),
        ],
    )
    return [outs[2 * i : 2 * i + 2] for i in range(len(sets))]


def ready_kernel(ids_ref, owner_ref, slot_ref, wavelet_ref, weights_ref, rows_ref):
    def pick(row, carry):
        weights_ref[pl.ds(row, 1), :] = wavelet_ref[pl.ds(ids_ref[row], 1), :]
        return carry

    lax.fori_loop(0, weights_ref.shape[0], pick, 0)

    def target(row, carry):
        rows_ref[row] = owner_ref[row] * MBLK + slot_ref[row]
        return carry

    lax.fori_loop(0, rows_ref.shape[0], target, 0)


def ready(ids, owner, slot, wavelet, after):
    return call(
        ready_kernel,
        "ready",
        [(SMEM, ids), (SMEM, owner), (SMEM, slot), (VMEM, wavelet)],
        [floats(*wavelet.shape), jax.ShapeDtypeStruct(slot.shape, jnp.int32)],
        [VMEM, SMEM],
        after,
    )


def join_kernel(mine_ref, arrived_ref, *refs, count):
    outs = refs[len(refs) - count :]
    last = mine_ref.shape[0] - 1
    outs[0][...] = mine_ref[0] + arrived_ref[0]
    outs[1][...] = mine_ref[last] + arrived_ref[last]
    if count == 3:
        outs[2][...] = refs[0][...]


def join(mine, arrived, following, after):
    count = 2 + len(following)
    return call(
        lambda *refs: join_kernel(*refs, count=count),
        "join",
        [(VMEM, value) for value in (mine, arrived, *following)],
        [floats(*mine.shape[1:])] * 2 + [floats(*value.shape) for value in following],
        [VMEM] * count,
        after,
    )


def gate_kernel(*refs):
    count = len(refs) // 2
    for value, out in zip(refs[:count], refs[count:]):
        out[...] = value[...]


def gate(values, after):
    return call(
        gate_kernel,
        "gate",
        [(VMEM, value) for value in values],
        [floats(*value.shape) for value in values],
        [VMEM] * len(values),
        after,
    )


def add_kernel(one_ref, two_ref, out_ref):
    out_ref[...] = one_ref[...] + two_ref[...]


def add(one, two, after):
    return call(add_kernel, "add", [(VMEM, one), (VMEM, two)], floats(*one.shape), VMEM, after)


def source_kernel(one_ref, two_ref, weights_ref, out_ref):
    weight_re, weight_im = weights_ref[:, 0:1], weights_ref[:, 1:2]
    real, imag = one_ref[0] + two_ref[0], one_ref[1] + two_ref[1]
    out_ref[0] = weight_re * real - weight_im * imag
    out_ref[1] = weight_re * imag + weight_im * real


def source(one, two, weights, after):
    return call(
        source_kernel,
        "source",
        [(VMEM, one), (VMEM, two), (VMEM, weights)],
        floats(*one.shape),
        VMEM,
        after,
    )


def cleave_kernel(field_ref, *outs):
    rows = outs[0].shape[1]
    for number, out in enumerate(outs):
        out[...] = field_ref[:, number * rows : (number + 1) * rows]


def cleave(field, streams, after):
    parts, shots, trace = field.shape
    return call(
        cleave_kernel,
        "cleave",
        [(VMEM, field)],
        [floats(parts, shots // streams, trace)] * streams,
        [VMEM] * streams,
        after,
    )


def step_kernel(me_ref, arrived_ref, high_ref, low_ref, own_ref, old_ref, out_ref, *, at, cut):
    active = lax.rem(me_ref[0], 2) == 0 if at is None else me_ref[0] == at

    @pl.when(active)
    def _():
        real, imag = product(arrived_ref[...], high_ref[...], low_ref[...])
        out_ref[0] = real + own_ref[0, cut]
        out_ref[1] = imag + own_ref[1, cut]

    @pl.when(jnp.logical_not(active))
    def _():
        out_ref[...] = old_ref[...]


def step(name, me, at, arrived, panel, own, first, old, after):
    cut = slice(first, first + old.shape[1])
    return call(
        lambda *refs: step_kernel(*refs, at=at, cut=cut),
        name,
        [(SMEM, me)] + [(VMEM, value) for value in (arrived, *panel, own, old)],
        floats(*old.shape),
        VMEM,
        after,
    )


def finish_kernel(me_ref, *refs, streams, width):
    arrived, owns, olds = (refs[i * streams : (i + 1) * streams] for i in range(3))
    high_ref, low_ref, out_ref, head_ref, tail_ref = refs[3 * streams :]
    trace = out_ref.shape[-1]

    @pl.when(lax.rem(me_ref[0], 2) == 1)
    def _():
        field = jnp.concatenate([ref[...] for ref in arrived], axis=1)
        real, imag = product(field, high_ref[...], low_ref[...])
        out_ref[0] = real + jnp.concatenate([ref[0] for ref in owns], axis=0)
        out_ref[1] = imag + jnp.concatenate([ref[1] for ref in owns], axis=0)

    @pl.when(lax.rem(me_ref[0], 2) == 0)
    def _():
        out_ref[...] = jnp.concatenate([ref[...] for ref in olds], axis=1)

    head_ref[...] = out_ref[:, :, :width]
    tail_ref[...] = out_ref[:, :, trace - width :]


def finish(me, arrived, panel, own, old, width, after):
    streams = len(own)
    _, rows, trace = own[0].shape
    shots = rows * streams
    return call(
        lambda *refs: finish_kernel(*refs, streams=streams, width=width),
        "finish",
        [(SMEM, me)] + [(VMEM, value) for value in (*arrived, *own, *old, *panel)],
        [floats(2, shots, trace), floats(2, shots, width), floats(2, shots, width)],
        [VMEM] * 3,
        after,
    )


def middle_kernel(field_ref, high_ref, low_ref, forward_ref, out_ref, *, width):
    inner = slice(width, width + field_ref.shape[-1])
    real, imag = product(field_ref[...], high_ref[inner], low_ref[inner])
    total = forward_ref[0] * real + forward_ref[1] * imag
    out_ref[...] = jnp.sum(total, axis=0, keepdims=True)


def middle(field, maps, forward, width):
    return call(
        lambda *refs: middle_kernel(*refs, width=width),
        "middle",
        [(VMEM, value) for value in (field, *maps, forward)],
        floats(1, forward.shape[-1]),
        VMEM,
        (),
        4 * 10**9,
    )


def rim_kernel(rows_ref, part_ref, left_ref, right_ref, high_ref, low_ref, forward_ref, out_ref):
    shots, width = left_ref.shape[1], left_ref.shape[2]
    depth = high_ref.shape[0]

    def ends(ref):
        return jnp.concatenate([ref[:width], ref[depth - width :]], axis=0)

    field = jnp.concatenate([left_ref[...], right_ref[...]], axis=-1)
    real, imag = product(field, ends(high_ref), ends(low_ref))
    total = forward_ref[0] * real + forward_ref[1] * imag
    gradient = part_ref[...] + jnp.sum(total, axis=0, keepdims=True)
    gradient = gradient * shots ** (-0.5)
    out_ref[...] = jnp.zeros_like(out_ref)
    for block in range(gradient.shape[1] // width):
        row = rows_ref[block]
        out_ref[pl.ds(row, 1), :] += gradient[:, block * width : (block + 1) * width]


def rim(rows, part, left, right, maps, forward, slabs):
    return call(
        rim_kernel,
        "rim",
        [(SMEM, rows)] + [(VMEM, value) for value in (part, left, right, *maps, forward)],
        floats(slabs * MBLK, left.shape[2]),
        VMEM,
        (),
    )


def body(
    residual_blocks,
    residual_slab,
    residual_pos,
    shot_ids,
    wavelet,
    down_panel,
    up_panel,
    recovery,
    forward_field,
    element_owner,
    element_slot,
):
    slabs = lax.axis_size("slab")
    lats = lax.axis_size("lat")
    groups = slabs // 2
    shots, width = residual_blocks.shape[2:]
    trace = down_panel.shape[-1]
    streams = 2 if shots % 32 == 0 else 1
    lanes = range(streams)
    rows = shots // streams
    me = lax.axis_index("slab").astype(jnp.int32).reshape(1)
    quads = slabs // 4
    sets = [(2, 0), (2, 1)] + [(4, quad) for quad in range(1, quads)]
    hops = quads.bit_length() - 1
    swapping = [(s, s ^ 1) for s in range(slabs)]

    def hop(value, route):
        return lax.ppermute(value, "slab", route)

    def toward(number, turn):
        size, which = sets[number]
        if turn == 0 and number != 1:
            return [(s, s ^ 2) for s in range(slabs)]
        bit = 1 << (turn if size == 2 else turn - 1)
        return [
            (s, s ^ (size * bit)) for s in range(slabs) if ((s // size) ^ which) & (2 * bit - 1) == bit
        ]

    def gather(which, after):
        return collect(
            me, residual_slab[:, 0], residual_pos, residual_blocks, which, trace, after
        )

    parts = gather(sets[:1], [])
    swapped = [hop(parts[0][1], swapping)]
    weights, targets = ready(shot_ids, element_owner[:, 0], element_slot, wavelet, [parts[0][0]])
    down = halves(down_panel[0, 0], [weights])
    parts += gather(sets[1:], [down[0]])
    total, sent, base = {}, {}, {}

    def stage_join(number, token):
        following = [part[1] for part in parts[number + 1 : number + 2]] if number >= 2 else []
        keep, joined, *gate = join(parts[number][0], swapped[number], following, token)
        total[number] = keep
        sent[number] = hop(joined, toward(number, 0))
        swapped.extend(hop(value, swapping) for value in gate)
        return [keep]

    def stage_add(number, turn, token):
        total[number] = add(total[number], sent[number], token)
        sent[number] = hop(total[number], toward(number, turn))
        return [total[number]]

    def stage_source(number, token):
        base[number] = source(total[number], sent[number], weights, token)
        return [base[number]]

    token = stage_join(0, [parts[1][0]])
    let = gate([part[1] for part in parts[1:3]], token)
    swapped += [hop(value, swapping) for value in let]
    token = let[:1]
    for turn in range(1, hops + 1):
        token = stage_add(0, turn, token)
    up = halves(up_panel[0, 0], token)
    maps = halves(recovery[0, 0], [up[0]])
    early = hold(me, 1, up_panel[0, 0], [maps[0]])
    early_panel = hop(early, [(p + 1, p) for p in range(0, slabs - 2, 4)])
    token = stage_join(1, [early])
    token = stage_source(0, token)
    state = list(cleave(base[0], streams, token))
    token = [state[0]]
    arrived = [hop(state[t], [(0, 1)]) for t in lanes]
    for s in range(1, slabs):
        number = s // 2 if s < 4 else s // 4 + 1
        for t in lanes:
            state[t] = step("down", me, s, arrived[t], down, base[number], t * rows, state[t], token)
            token = [state[t]]
        if s + 1 < slabs:
            arrived = [hop(state[t], [(s, s + 1)]) for t in lanes]
        else:
            beside = [hop(state[t], [(p + 1, p) for p in range(0, slabs, 2)]) for t in lanes]
        if s == 1:
            for turn in range(1, hops + 1):
                token = stage_add(1, turn, token)
        number = s // 4 + 2
        if number < len(sets):
            if s % 4 == 1:
                token = stage_join(number, token)
            if s % 4 == 2:
                for turn in range(1, hops + 1):
                    token = stage_add(number, turn, token)
            if s % 4 == 3:
                token = stage_source(number, token)
        if s == 1:
            late = hold(me, 3, up_panel[0, 0], token)
            late_panel = hop(late, [(p + 1, p) for p in range(2, slabs - 2, 4)])
            token = stage_source(1, [late])
    local = []
    for t in lanes:
        local.append(step("local", me, None, beside[t], up, state[t], 0, state[t], token))
        token = [local[t]]
    above = list(local)
    arrived = [hop(above[t], [(slabs - 2, slabs - 4)]) for t in lanes]
    pair = pair_panel(me, early_panel, late_panel, up, token, slabs - 2)
    token = [pair[0]]
    for p in range(slabs - 4, -1, -2):
        if p == 0:
            after = [hop(above[t], [(q + 2, q + 1) for q in range(0, slabs - 2, 2)]) for t in lanes]
        for t in lanes:
            above[t] = step("up", me, p, arrived[t], pair, local[t], 0, above[t], token)
            token = [above[t]]
        if p > 0:
            arrived = [hop(above[t], [(p, p - 2)]) for t in lanes]
    ups, head, tail = finish(me, after, up, state, above, width, token)

    left = lax.ppermute(tail, "lat", [(i, i + 1) for i in range(lats - 1)])
    right = lax.ppermute(head, "lat", [(i + 1, i) for i in range(lats - 1)])
    part = middle(ups, maps, forward_field[0, 0], width)
    outgoing = rim(targets, part, left, right, maps, forward_field[0, 0], slabs)
    arrived = lax.all_to_all(outgoing, "slab", split_axis=0, concat_axis=0, tiled=True)
    model = jnp.sum(arrived.reshape(slabs, MBLK, width), axis=0)
    return (ups[None, None], model[None, None])


def solution(mesh):
    placed = (
        P(("slab", "lat"), None, None, None),
        P(("slab", "lat"), None),
        P(("slab", "lat")),
        P(),
        P(),
        P("slab", "lat", None, None, None),
        P("slab", "lat", None, None, None),
        P("slab", "lat", None, None, None),
        P("slab", "lat", None, None, None),
        P(("slab", "lat"), None),
        P(("slab", "lat")),
    )
    return jax.shard_map(
        body,
        mesh=mesh,
        in_specs=placed,
        out_specs=(P("slab", "lat", None, None, None), P("slab", "lat", None, None)),
        check_vma=False,
    )
```

```python
import jax
import jax.numpy as jnp
from jax import lax
from jax.experimental import pallas as pl
from jax.experimental.pallas import tpu as pltpu
from jax.sharding import PartitionSpec as P

MBLK = 8
VMEM = pl.BlockSpec(memory_space=pltpu.VMEM)
SMEM = pl.BlockSpec(memory_space=pltpu.SMEM)
ANY = pl.BlockSpec(memory_space=pl.ANY)
HBM = pl.BlockSpec(memory_space=pltpu.HBM)
CHUNKS = 4


def floats(*shape):
    return jax.ShapeDtypeStruct(shape, jnp.float32)


def cost(flops):
    return pl.CostEstimate(flops=flops, bytes_accessed=flops // 1000, transcendentals=0)


def split(value):
    high = value.astype(jnp.bfloat16)
    low = (value - high.astype(jnp.float32)).astype(jnp.bfloat16)
    return high, low


def product(vector, high, low):
    m, n = vector.shape[1], high.shape[1] // 2
    top, rest = split(vector.reshape(2 * m, -1))
    wide = jnp.dot(top, high, preferred_element_type=jnp.float32)
    wide += jnp.dot(rest, high, preferred_element_type=jnp.float32)
    wide += jnp.dot(top, low, preferred_element_type=jnp.float32)
    return wide[:m, :n] - wide[m:, n:], wide[:m, n:] + wide[m:, :n]


def call(kernel, name, ins, outs, out_specs, after, flops=0, room=16, **keywords):
    specs, values = zip(*ins)
    count = len(values)

    def run(*refs):
        kernel(*refs[:count], *refs[count + len(after) :])

    return pl.pallas_call(
        run,
        in_specs=list(specs) + [ANY] * len(after),
        out_specs=out_specs,
        out_shape=outs,
        compiler_params=pltpu.CompilerParams(vmem_limit_bytes=room * 1024 * 1024),
        cost_estimate=cost(flops) if flops else None,
        name=name,
        **keywords,
    )(*values, *after)


def halves_kernel(panel_ref, high_ref, low_ref):
    n = panel_ref.shape[-1]
    for part in range(2):
        high, low = split(panel_ref[part])
        high_ref[:, part * n : (part + 1) * n] = high
        low_ref[:, part * n : (part + 1) * n] = low


def halves(panel, after, rows=128):
    _, k, n = panel.shape
    block = pl.BlockSpec((rows, 2 * n), lambda i: (i, 0))
    return call(
        halves_kernel,
        "halves",
        [(pl.BlockSpec((2, rows, n), lambda i: (0, i, 0)), panel)],
        [jax.ShapeDtypeStruct((k, 2 * n), jnp.bfloat16)] * 2,
        [block, block],
        after,
        2 * 10**9,
        grid=(k // rows,),
    )


def either_kernel(me_ref, near_ref, far_ref, high_ref, low_ref):
    @pl.when(me_ref[0] < 2)
    def _():
        halves_kernel(near_ref, high_ref, low_ref)

    @pl.when(me_ref[0] >= 2)
    def _():
        halves_kernel(far_ref, high_ref, low_ref)


def halves_of_two(me, near, far, after, rows=128):
    _, k, n = near.shape
    piece = pl.BlockSpec((2, rows, n), lambda i: (0, i, 0))
    block = pl.BlockSpec((rows, 2 * n), lambda i: (i, 0))
    return call(
        either_kernel,
        "halves",
        [(SMEM, me), (piece, near), (piece, far)],
        [jax.ShapeDtypeStruct((k, 2 * n), jnp.bfloat16)] * 2,
        [block, block],
        after,
        grid=(k // rows,),
    )


def hold_kernel(me_ref, panel_ref, out_ref, *, least):
    slab = me_ref[0]

    @pl.when((lax.rem(slab, 2) == 1) & ((slab >= least) if least > 1 else (slab == least)))
    def _():
        out_ref[...] = panel_ref[...]


def hold(me, least, panel, after):
    return call(
        lambda *refs: hold_kernel(*refs, least=least),
        "hold",
        [(SMEM, me), (VMEM, panel)],
        floats(*panel.shape),
        VMEM,
        after,
    )


def collect_kernel(me_ref, slab_hbm, pos_hbm, blocks_hbm, *refs, sets):
    outs, (slab_ref, pos_ref, blocks_ref, sems) = refs[:-4], refs[-4:]
    count, width = blocks_ref.shape[0], blocks_ref.shape[-1]
    chunk = count // CHUNKS
    me = me_ref[0]
    copies = [
        pltpu.make_async_copy(slab_hbm, slab_ref, sems.at[CHUNKS]),
        pltpu.make_async_copy(pos_hbm, pos_ref, sems.at[CHUNKS + 1]),
    ]
    for i in range(CHUNKS):
        some = pl.ds(i * chunk, chunk)
        copies.append(pltpu.make_async_copy(blocks_hbm.at[some], blocks_ref.at[some], sems.at[i]))
    for copy in copies:
        copy.start()
    for out in outs:
        out[...] = jnp.zeros_like(out)
    copies[0].wait()
    copies[1].wait()

    def place(row, carry):
        slab = slab_ref[row]
        apart = lax.bitwise_xor(slab, me)
        side = lax.rem(apart, 2)
        lanes = pl.ds(pl.multiple_of(pos_ref[row] * width, width), width)
        for number, (size, which) in enumerate(sets):
            turn = lax.rem(lax.div(apart, 2), 2) if size == 4 else 0
            for other in range(2):

                @pl.when((lax.div(slab, size) == which) & (side == other))
                def _():
                    for part in range(2):
                        outs[2 * number + other][turn, part, :, lanes] += blocks_ref[row, part]

        return carry

    for i in range(CHUNKS):
        copies[2 + i].wait()
        lax.fori_loop(i * chunk, (i + 1) * chunk, place, 0)


def collect(me, slab, pos, blocks, sets, trace, after):
    shots = blocks.shape[2]
    shapes = [floats(size // 2, 2, shots, trace) for size, _ in sets for _ in range(2)]
    outs = call(
        lambda *refs: collect_kernel(*refs, sets=sets),
        "collect",
        [(SMEM, me), (HBM, slab), (HBM, pos), (HBM, blocks)],
        shapes,
        [VMEM] * len(shapes),
        after,
        2 * 10**9,
        59 if not after else 16,
        scratch_shapes=[
            pltpu.SMEM(slab.shape, jnp.int32),
            pltpu.SMEM(pos.shape, jnp.int32),
            pltpu.VMEM(blocks.shape, jnp.float32),
            pltpu.SemaphoreType.DMA((CHUNKS + 2,)),
        ],
    )
    return [outs[2 * i : 2 * i + 2] for i in range(len(sets))]


def ready_kernel(ids_ref, owner_ref, slot_ref, wavelet_ref, weights_ref, rows_ref):
    def pick(row, carry):
        weights_ref[pl.ds(row, 1), :] = wavelet_ref[pl.ds(ids_ref[row], 1), :]
        return carry

    lax.fori_loop(0, weights_ref.shape[0], pick, 0)

    def target(row, carry):
        rows_ref[row] = owner_ref[row] * MBLK + slot_ref[row]
        return carry

    lax.fori_loop(0, rows_ref.shape[0], target, 0)


def ready(ids, owner, slot, wavelet, after):
    return call(
        ready_kernel,
        "ready",
        [(SMEM, ids), (SMEM, owner), (SMEM, slot), (VMEM, wavelet)],
        [floats(*wavelet.shape), jax.ShapeDtypeStruct(slot.shape, jnp.int32)],
        [VMEM, SMEM],
        after,
    )


def join_kernel(mine_ref, arrived_ref, *refs, count):
    outs = refs[len(refs) - count :]
    last = mine_ref.shape[0] - 1
    outs[0][...] = mine_ref[0] + arrived_ref[0]
    outs[1][...] = mine_ref[last] + arrived_ref[last]
    if count == 3:
        outs[2][...] = refs[0][...]


def join(mine, arrived, following, after):
    count = 2 + len(following)
    return call(
        lambda *refs: join_kernel(*refs, count=count),
        "join",
        [(VMEM, value) for value in (mine, arrived, *following)],
        [floats(*mine.shape[1:])] * 2 + [floats(*value.shape) for value in following],
        [VMEM] * count,
        after,
    )


def gate_kernel(*refs):
    count = len(refs) // 2
    for value, out in zip(refs[:count], refs[count:]):
        out[...] = value[...]


def gate(values, after):
    return call(
        gate_kernel,
        "gate",
        [(VMEM, value) for value in values],
        [floats(*value.shape) for value in values],
        [VMEM] * len(values),
        after,
    )


def add_kernel(one_ref, two_ref, out_ref):
    out_ref[...] = one_ref[...] + two_ref[...]


def add(one, two, after):
    return call(add_kernel, "add", [(VMEM, one), (VMEM, two)], floats(*one.shape), VMEM, after)


def source_kernel(one_ref, two_ref, weights_ref, out_ref):
    weight_re, weight_im = weights_ref[:, 0:1], weights_ref[:, 1:2]
    real, imag = one_ref[0] + two_ref[0], one_ref[1] + two_ref[1]
    out_ref[0] = weight_re * real - weight_im * imag
    out_ref[1] = weight_re * imag + weight_im * real


def source(one, two, weights, after):
    return call(
        source_kernel,
        "source",
        [(VMEM, one), (VMEM, two), (VMEM, weights)],
        floats(*one.shape),
        VMEM,
        after,
    )


def cleave_kernel(field_ref, *outs):
    rows = outs[0].shape[1]
    for number, out in enumerate(outs):
        out[...] = field_ref[:, number * rows : (number + 1) * rows]


def cleave(field, streams, after):
    parts, shots, trace = field.shape
    return call(
        cleave_kernel,
        "cleave",
        [(VMEM, field)],
        [floats(parts, shots // streams, trace)] * streams,
        [VMEM] * streams,
        after,
    )


def step_kernel(me_ref, arrived_ref, high_ref, low_ref, own_ref, old_ref, out_ref, *, at, cut):
    active = me_ref[0] == at

    @pl.when(active)
    def _():
        arrived = arrived_ref[...] if arrived_ref.shape == out_ref.shape else arrived_ref[:, cut]
        real, imag = product(arrived, high_ref[...], low_ref[...])
        own = own_ref[...] if own_ref.shape == out_ref.shape else own_ref[:, cut]
        out_ref[0] = real + own[0]
        out_ref[1] = imag + own[1]

    @pl.when(jnp.logical_not(active))
    def _():
        out_ref[...] = old_ref[...]


def step(name, me, at, arrived, panel, own, first, old, after):
    cut = slice(first, first + old.shape[1])
    return call(
        lambda *refs: step_kernel(*refs, at=at, cut=cut),
        name,
        [(SMEM, me)] + [(VMEM, value) for value in (arrived, *panel, own, old)],
        floats(*old.shape),
        VMEM,
        after,
    )


def up_kernel(me_ref, arrived_ref, oh, ol, beside_ref, eh, el, own_ref, old_ref, out_ref, *, at):
    @pl.when(me_ref[0] == at)
    def _():
        real, imag = product(arrived_ref[...], oh[...], ol[...])
        out_ref[0] = real + beside_ref[0]
        out_ref[1] = imag + beside_ref[1]
        real, imag = product(out_ref[...], eh[...], el[...])
        out_ref[0] = real + own_ref[0]
        out_ref[1] = imag + own_ref[1]

    @pl.when(me_ref[0] != at)
    def _():
        out_ref[...] = old_ref[...]


def up_step(me, at, arrived, odd, beside, even, own, old, after):
    return call(
        lambda *refs: up_kernel(*refs, at=at),
        "up",
        [(SMEM, me)] + [(VMEM, value) for value in (arrived, *odd, beside, *even, own, old)],
        floats(*own.shape),
        VMEM,
        after,
    )


def whole(refs):
    return jnp.concatenate([ref[...] for ref in refs], axis=1)


def edges_kernel(me_ref, *refs, streams, width):
    arrived, owns, olds = (refs[i * streams : (i + 1) * streams] for i in range(3))
    high_ref, low_ref, head_ref, tail_ref = refs[3 * streams :]
    trace = high_ref.shape[1] // 2
    first, last = slice(0, width), slice(trace - width, trace)
    passed = lax.rem(me_ref[0], 2) == 1

    def ends(ref):
        more = (slice(trace, trace + width), slice(2 * trace - width, 2 * trace))
        return jnp.concatenate([ref[:, cut] for cut in (first, last, *more)], axis=1)

    @pl.when(passed)
    def _():
        values = product(whole(arrived), ends(high_ref), ends(low_ref))
        own = whole(owns)
        for part, value in enumerate(values):
            head_ref[part] = value[:, :width] + own[part, :, first]
            tail_ref[part] = value[:, width:] + own[part, :, last]

    @pl.when(jnp.logical_not(passed))
    def _():
        old = whole(olds)
        head_ref[...] = old[:, :, first]
        tail_ref[...] = old[:, :, last]


def edges(me, arrived, panel, own, old, width, after):
    streams = len(own)
    shots = own[0].shape[1] * streams
    return call(
        lambda *refs: edges_kernel(*refs, streams=streams, width=width),
        "edges",
        [(SMEM, me)] + [(VMEM, value) for value in (*arrived, *own, *old, *panel)],
        [floats(2, shots, width)] * 2,
        [VMEM] * 2,
        after,
    )


def finish_kernel(me_ref, *refs, streams):
    arrived, owns, olds = (refs[i * streams : (i + 1) * streams] for i in range(3))
    high_ref, low_ref, out_ref, again_ref = refs[3 * streams :]
    passed = lax.rem(me_ref[0], 2) == 1

    @pl.when(passed)
    def _():
        real, imag = product(whole(arrived), high_ref[...], low_ref[...])
        own = whole(owns)
        out_ref[0] = real + own[0]
        out_ref[1] = imag + own[1]

    @pl.when(jnp.logical_not(passed))
    def _():
        out_ref[...] = whole(olds)

    again_ref[...] = out_ref[...]


def finish(me, arrived, panel, own, old, after):
    streams = len(own)
    _, rows, trace = own[0].shape
    return call(
        lambda *refs: finish_kernel(*refs, streams=streams),
        "finish",
        [(SMEM, me)] + [(VMEM, value) for value in (*arrived, *own, *old, *panel)],
        [floats(2, rows * streams, trace)] * 2,
        [VMEM] * 2,
        after,
    )


def middle_kernel(field_ref, high_ref, low_ref, forward_ref, out_ref, *, width):
    inner = slice(width, width + field_ref.shape[-1])
    real, imag = product(field_ref[...], high_ref[inner], low_ref[inner])
    total = forward_ref[0] * real + forward_ref[1] * imag
    out_ref[...] = jnp.sum(total, axis=0, keepdims=True)


def middle(field, maps, forward, width):
    return call(
        lambda *refs: middle_kernel(*refs, width=width),
        "middle",
        [(VMEM, value) for value in (field, *maps, forward)],
        floats(1, forward.shape[-1]),
        VMEM,
        (),
    )


def rim_kernel(rows_ref, part_ref, left_ref, right_ref, high_ref, low_ref, forward_ref, out_ref):
    shots, width = left_ref.shape[1], left_ref.shape[2]
    depth = high_ref.shape[0]

    def ends(ref):
        return jnp.concatenate([ref[:width], ref[depth - width :]], axis=0)

    field = jnp.concatenate([left_ref[...], right_ref[...]], axis=-1)
    real, imag = product(field, ends(high_ref), ends(low_ref))
    total = forward_ref[0] * real + forward_ref[1] * imag
    gradient = part_ref[...] + jnp.sum(total, axis=0, keepdims=True)
    gradient = gradient * shots ** (-0.5)
    out_ref[...] = jnp.zeros_like(out_ref)
    for block in range(gradient.shape[1] // width):
        row = rows_ref[block]
        out_ref[pl.ds(row, 1), :] += gradient[:, block * width : (block + 1) * width]


def rim(rows, part, left, right, maps, forward, slabs):
    return call(
        rim_kernel,
        "rim",
        [(SMEM, rows)] + [(VMEM, value) for value in (part, left, right, *maps, forward)],
        floats(slabs * MBLK, left.shape[2]),
        VMEM,
        (),
    )


def body(
    residual_blocks,
    residual_slab,
    residual_pos,
    shot_ids,
    wavelet,
    down_panel,
    up_panel,
    recovery,
    forward_field,
    element_owner,
    element_slot,
):
    slabs = lax.axis_size("slab")
    lats = lax.axis_size("lat")
    groups = slabs // 2
    shots, width = residual_blocks.shape[2:]
    trace = down_panel.shape[-1]
    streams = 2 if shots % 32 == 0 else 1
    lanes = range(streams)
    rows = shots // streams
    me = lax.axis_index("slab").astype(jnp.int32).reshape(1)
    quads = slabs // 4
    sets = [(2, 0), (2, 1)] + [(4, quad) for quad in range(1, quads)]
    hops = quads.bit_length() - 1
    swapping = [(s, s ^ 1) for s in range(slabs)]

    def hop(value, route):
        return lax.ppermute(value, "slab", route)

    def toward(number, turn):
        size, which = sets[number]
        if turn == 0 and number != 1:
            return [(s, s ^ 2) for s in range(slabs)]
        bit = 1 << (turn if size == 2 else turn - 1)
        return [
            (s, s ^ (size * bit)) for s in range(slabs) if ((s // size) ^ which) & (2 * bit - 1) == bit
        ]

    def gather(which, after):
        return collect(
            me, residual_slab[:, 0], residual_pos, residual_blocks, which, trace, after
        )

    parts = gather(sets[:1], [])
    swapped = [hop(parts[0][1], swapping)]
    weights, targets = ready(shot_ids, element_owner[:, 0], element_slot, wavelet, [parts[0][0]])
    down = halves(down_panel[0, 0], [weights])
    parts += gather(sets[1:], [down[0]])
    total, sent, base = {}, {}, {}

    def stage_join(number, token):
        following = [part[1] for part in parts[number + 1 : number + 2]] if number >= 2 else []
        keep, joined, *gate = join(parts[number][0], swapped[number], following, token)
        total[number] = keep
        sent[number] = hop(joined, toward(number, 0))
        swapped.extend(hop(value, swapping) for value in gate)
        return [keep]

    def stage_add(number, turn, token):
        total[number] = add(total[number], sent[number], token)
        sent[number] = hop(total[number], toward(number, turn))
        return [total[number]]

    def stage_source(number, token):
        base[number] = source(total[number], sent[number], weights, token)
        return [base[number]]

    token = stage_join(0, [parts[1][0]])
    let = gate([part[1] for part in parts[1:3]], token)
    swapped += [hop(value, swapping) for value in let]
    token = let[:1]
    for turn in range(1, hops + 1):
        token = stage_add(0, turn, token)
    token = stage_join(1, token)
    up = halves(up_panel[0, 0], token)
    maps = halves(recovery[0, 0], [up[0]])
    held = hold(me, 3, up_panel[0, 0], [maps[0]])
    far_panel = hop(held, [(p + 1, p) for p in range(2, slabs - 2, 2)])
    token = stage_source(0, [held])
    arrived = hop(base[0], [(0, 1)])
    for turn in range(1, hops + 1):
        token = stage_add(1, turn, token)
    token = stage_join(2, token)
    whole = step("down", me, 1, arrived, down, base[0], 0, base[0], token)
    arrived = [hop(whole, [(1, 2)])] * streams
    state = list(cleave(whole, streams, [whole]))
    token = stage_source(1, state[:1])
    for turn in range(1, hops + 1):
        token = stage_add(2, turn, token)
    held = hold(me, 1, up_panel[0, 0], token + arrived[:1])
    near_panel = hop(held, [(1, 0)])
    token = [held]
    for s in range(2, slabs):
        number = s // 2 if s < 4 else s // 4 + 1
        for t in lanes:
            state[t] = step("down", me, s, arrived[t], down, base[number], t * rows, state[t], token)
            token = [state[t]]
        if s + 1 < slabs:
            arrived = [hop(state[t], [(s, s + 1)]) for t in lanes]
        else:
            arrived = [hop(state[t], [(s, s - 1)]) for t in lanes]
            beside = [hop(state[t], [(p + 1, p) for p in range(0, slabs - 2, 2)]) for t in lanes]
        number = s // 4 + 2
        if number < len(sets):
            if s % 4 == 1:
                token = stage_join(number, token)
            if s % 4 == 2 and s > 2:
                for turn in range(1, hops + 1):
                    token = stage_add(number, turn, token)
            if s % 4 == 3:
                token = stage_source(number, token)
    above = list(state)
    for t in lanes:
        above[t] = step("up", me, slabs - 2, arrived[t], up, state[t], 0, above[t], token)
        token = [above[t]]
    arrived = [hop(above[t], [(slabs - 2, slabs - 4)]) for t in lanes]
    odd_up = halves_of_two(me, near_panel, far_panel, token)
    token = [odd_up[0]]
    for p in range(slabs - 4, -1, -2):
        if p == 0:
            after = [hop(above[t], [(q + 2, q + 1) for q in range(0, slabs - 2, 2)]) for t in lanes]
        for t in lanes:
            above[t] = up_step(
                me, p, arrived[t], odd_up, beside[t], up, state[t], above[t], token
            )
            token = [above[t]]
        if p > 0:
            arrived = [hop(above[t], [(p, p - 2)]) for t in lanes]
    head, tail = edges(me, after, up, state, above, width, token)
    left = lax.ppermute(tail, "lat", [(i, i + 1) for i in range(lats - 1)])
    right = lax.ppermute(head, "lat", [(i + 1, i) for i in range(lats - 1)])
    ups, field = finish(me, after, up, state, above, [head])
    part = middle(field, maps, forward_field[0, 0], width)
    outgoing = rim(targets, part, left, right, maps, forward_field[0, 0], slabs)
    arrived = lax.all_to_all(outgoing, "slab", split_axis=0, concat_axis=0, tiled=True)
    model = jnp.sum(arrived.reshape(slabs, MBLK, width), axis=0)
    return (ups[None, None], model[None, None])


def solution(mesh):
    placed = (
        P(("slab", "lat"), None, None, None),
        P(("slab", "lat"), None),
        P(("slab", "lat")),
        P(),
        P(),
        P("slab", "lat", None, None, None),
        P("slab", "lat", None, None, None),
        P("slab", "lat", None, None, None),
        P("slab", "lat", None, None, None),
        P(("slab", "lat"), None),
        P(("slab", "lat")),
    )
    return jax.shard_map(
        body,
        mesh=mesh,
        in_specs=placed,
        out_specs=(P("slab", "lat", None, None, None), P("slab", "lat", None, None)),
        check_vma=False,
    )
```

```python
import jax
import jax.numpy as jnp
from jax import lax
from jax.experimental import pallas as pl
from jax.experimental.pallas import tpu as pltpu
from jax.sharding import PartitionSpec as P

MBLK = 8
VMEM = pl.BlockSpec(memory_space=pltpu.VMEM)
SMEM = pl.BlockSpec(memory_space=pltpu.SMEM)
ANY = pl.BlockSpec(memory_space=pl.ANY)
HBM = pl.BlockSpec(memory_space=pltpu.HBM)
CHUNKS = 4


def floats(*shape):
    return jax.ShapeDtypeStruct(shape, jnp.float32)


def cost(flops):
    return pl.CostEstimate(flops=flops, bytes_accessed=flops // 1000, transcendentals=0)


def split(value):
    high = value.astype(jnp.bfloat16)
    low = (value - high.astype(jnp.float32)).astype(jnp.bfloat16)
    return high, low


def product(vector, high, low):
    m, n = vector.shape[1], high.shape[1] // 2
    top, rest = split(vector.reshape(2 * m, -1))
    wide = jnp.dot(top, high, preferred_element_type=jnp.float32)
    wide += jnp.dot(rest, high, preferred_element_type=jnp.float32)
    wide += jnp.dot(top, low, preferred_element_type=jnp.float32)
    return wide[:m, :n] - wide[m:, n:], wide[:m, n:] + wide[m:, :n]


def call(kernel, name, ins, outs, out_specs, after, flops=0, room=16, **keywords):
    specs, values = zip(*ins)
    count = len(values)

    def run(*refs):
        kernel(*refs[:count], *refs[count + len(after) :])

    return pl.pallas_call(
        run,
        in_specs=list(specs) + [ANY] * len(after),
        out_specs=out_specs,
        out_shape=outs,
        compiler_params=pltpu.CompilerParams(vmem_limit_bytes=room * 1024 * 1024),
        cost_estimate=cost(flops) if flops else None,
        name=name,
        **keywords,
    )(*values, *after)


def halves_kernel(panel_ref, high_ref, low_ref):
    n = panel_ref.shape[-1]
    for part in range(2):
        high, low = split(panel_ref[part])
        high_ref[:, part * n : (part + 1) * n] = high
        low_ref[:, part * n : (part + 1) * n] = low


def halves(panel, after, rows=128):
    _, k, n = panel.shape
    block = pl.BlockSpec((rows, 2 * n), lambda i: (i, 0))
    return call(
        halves_kernel,
        "halves",
        [(pl.BlockSpec((2, rows, n), lambda i: (0, i, 0)), panel)],
        [jax.ShapeDtypeStruct((k, 2 * n), jnp.bfloat16)] * 2,
        [block, block],
        after,
        2 * 10**9,
        grid=(k // rows,),
    )


def either_kernel(me_ref, near_ref, far_ref, high_ref, low_ref):
    @pl.when(me_ref[0] < 2)
    def _():
        halves_kernel(near_ref, high_ref, low_ref)

    @pl.when(me_ref[0] >= 2)
    def _():
        halves_kernel(far_ref, high_ref, low_ref)


def halves_of_two(me, near, far, after, rows=128):
    _, k, n = near.shape
    piece = pl.BlockSpec((2, rows, n), lambda i: (0, i, 0))
    block = pl.BlockSpec((rows, 2 * n), lambda i: (i, 0))
    return call(
        either_kernel,
        "halves",
        [(SMEM, me), (piece, near), (piece, far)],
        [jax.ShapeDtypeStruct((k, 2 * n), jnp.bfloat16)] * 2,
        [block, block],
        after,
        grid=(k // rows,),
    )


def hold_kernel(me_ref, panel_ref, out_ref, *, least):
    slab = me_ref[0]

    @pl.when((lax.rem(slab, 2) == 1) & ((slab >= least) if least > 1 else (slab == least)))
    def _():
        out_ref[...] = panel_ref[...]


def hold(me, least, panel, after):
    return call(
        lambda *refs: hold_kernel(*refs, least=least),
        "hold",
        [(SMEM, me), (VMEM, panel)],
        floats(*panel.shape),
        VMEM,
        after,
    )


def collect_kernel(me_ref, slab_hbm, pos_hbm, blocks_hbm, *refs, sets):
    outs, (slab_ref, pos_ref, blocks_ref, sems) = refs[:-4], refs[-4:]
    count, width = blocks_ref.shape[0], blocks_ref.shape[-1]
    chunk = count // CHUNKS
    me = me_ref[0]
    copies = [
        pltpu.make_async_copy(slab_hbm, slab_ref, sems.at[CHUNKS]),
        pltpu.make_async_copy(pos_hbm, pos_ref, sems.at[CHUNKS + 1]),
    ]
    for i in range(CHUNKS):
        some = pl.ds(i * chunk, chunk)
        copies.append(pltpu.make_async_copy(blocks_hbm.at[some], blocks_ref.at[some], sems.at[i]))
    for copy in copies:
        copy.start()
    for out in outs:
        out[...] = jnp.zeros_like(out)
    copies[0].wait()
    copies[1].wait()

    def place(row, carry):
        slab = slab_ref[row]
        apart = lax.bitwise_xor(slab, me)
        side = lax.rem(apart, 2)
        lanes = pl.ds(pl.multiple_of(pos_ref[row] * width, width), width)
        for number, (size, which) in enumerate(sets):
            turn = lax.rem(lax.div(apart, 2), 2) if size == 4 else 0
            for other in range(2):

                @pl.when((lax.div(slab, size) == which) & (side == other))
                def _():
                    for part in range(2):
                        outs[2 * number + other][turn, part, :, lanes] += blocks_ref[row, part]

        return carry

    for i in range(CHUNKS):
        copies[2 + i].wait()
        lax.fori_loop(i * chunk, (i + 1) * chunk, place, 0)


def collect(me, slab, pos, blocks, sets, trace, after):
    shots = blocks.shape[2]
    shapes = [floats(size // 2, 2, shots, trace) for size, _ in sets for _ in range(2)]
    outs = call(
        lambda *refs: collect_kernel(*refs, sets=sets),
        "collect",
        [(SMEM, me), (HBM, slab), (HBM, pos), (HBM, blocks)],
        shapes,
        [VMEM] * len(shapes),
        after,
        2 * 10**9,
        59 if not after else 16,
        scratch_shapes=[
            pltpu.SMEM(slab.shape, jnp.int32),
            pltpu.SMEM(pos.shape, jnp.int32),
            pltpu.VMEM(blocks.shape, jnp.float32),
            pltpu.SemaphoreType.DMA((CHUNKS + 2,)),
        ],
    )
    return [outs[2 * i : 2 * i + 2] for i in range(len(sets))]


def ready_kernel(ids_ref, owner_ref, slot_ref, wavelet_ref, weights_ref, rows_ref):
    def pick(row, carry):
        weights_ref[pl.ds(row, 1), :] = wavelet_ref[pl.ds(ids_ref[row], 1), :]
        return carry

    lax.fori_loop(0, weights_ref.shape[0], pick, 0)

    def target(row, carry):
        rows_ref[row] = owner_ref[row] * MBLK + slot_ref[row]
        return carry

    lax.fori_loop(0, rows_ref.shape[0], target, 0)


def ready(ids, owner, slot, wavelet, after):
    return call(
        ready_kernel,
        "ready",
        [(SMEM, ids), (SMEM, owner), (SMEM, slot), (VMEM, wavelet)],
        [floats(*wavelet.shape), jax.ShapeDtypeStruct(slot.shape, jnp.int32)],
        [VMEM, SMEM],
        after,
    )


def join_kernel(mine_ref, arrived_ref, *refs, count):
    outs = refs[len(refs) - count :]
    last = mine_ref.shape[0] - 1
    outs[0][...] = mine_ref[0] + arrived_ref[0]
    outs[1][...] = mine_ref[last] + arrived_ref[last]
    if count == 3:
        outs[2][...] = refs[0][...]


def join(mine, arrived, following, after):
    count = 2 + len(following)
    return call(
        lambda *refs: join_kernel(*refs, count=count),
        "join",
        [(VMEM, value) for value in (mine, arrived, *following)],
        [floats(*mine.shape[1:])] * 2 + [floats(*value.shape) for value in following],
        [VMEM] * count,
        after,
    )


def gate_kernel(*refs):
    count = len(refs) // 2
    for value, out in zip(refs[:count], refs[count:]):
        out[...] = value[...]


def gate(values, after):
    return call(
        gate_kernel,
        "gate",
        [(VMEM, value) for value in values],
        [floats(*value.shape) for value in values],
        [VMEM] * len(values),
        after,
    )


def add_kernel(one_ref, two_ref, out_ref):
    out_ref[...] = one_ref[...] + two_ref[...]


def add(one, two, after):
    return call(add_kernel, "add", [(VMEM, one), (VMEM, two)], floats(*one.shape), VMEM, after)


def source_kernel(one_ref, two_ref, weights_ref, out_ref):
    weight_re, weight_im = weights_ref[:, 0:1], weights_ref[:, 1:2]
    real, imag = one_ref[0] + two_ref[0], one_ref[1] + two_ref[1]
    out_ref[0] = weight_re * real - weight_im * imag
    out_ref[1] = weight_re * imag + weight_im * real


def source(one, two, weights, after):
    return call(
        source_kernel,
        "source",
        [(VMEM, one), (VMEM, two), (VMEM, weights)],
        floats(*one.shape),
        VMEM,
        after,
    )


def cleave_kernel(field_ref, *outs):
    rows = outs[0].shape[1]
    for number, out in enumerate(outs):
        out[...] = field_ref[:, number * rows : (number + 1) * rows]


def cleave(field, streams, after):
    parts, shots, trace = field.shape
    return call(
        cleave_kernel,
        "cleave",
        [(VMEM, field)],
        [floats(parts, shots // streams, trace)] * streams,
        [VMEM] * streams,
        after,
    )


def step_kernel(me_ref, arrived_ref, high_ref, low_ref, own_ref, old_ref, out_ref, *, at, cut):
    active = me_ref[0] == at

    @pl.when(active)
    def _():
        arrived = arrived_ref[...] if arrived_ref.shape == out_ref.shape else arrived_ref[:, cut]
        real, imag = product(arrived, high_ref[...], low_ref[...])
        own = own_ref[...] if own_ref.shape == out_ref.shape else own_ref[:, cut]
        out_ref[0] = real + own[0]
        out_ref[1] = imag + own[1]

    @pl.when(jnp.logical_not(active))
    def _():
        out_ref[...] = old_ref[...]


def step(name, me, at, arrived, panel, own, first, old, after):
    cut = slice(first, first + old.shape[1])
    return call(
        lambda *refs: step_kernel(*refs, at=at, cut=cut),
        name,
        [(SMEM, me)] + [(VMEM, value) for value in (arrived, *panel, own, old)],
        floats(*old.shape),
        VMEM,
        after,
    )


def up_kernel(me_ref, arrived_ref, oh, ol, beside_ref, eh, el, own_ref, old_ref, out_ref, *, at):
    @pl.when(me_ref[0] == at)
    def _():
        real, imag = product(arrived_ref[...], oh[...], ol[...])
        out_ref[0] = real + beside_ref[0]
        out_ref[1] = imag + beside_ref[1]
        real, imag = product(out_ref[...], eh[...], el[...])
        out_ref[0] = real + own_ref[0]
        out_ref[1] = imag + own_ref[1]

    @pl.when(me_ref[0] != at)
    def _():
        out_ref[...] = old_ref[...]


def up_step(me, at, arrived, odd, beside, even, own, old, after):
    return call(
        lambda *refs: up_kernel(*refs, at=at),
        "up",
        [(SMEM, me)] + [(VMEM, value) for value in (arrived, *odd, beside, *even, own, old)],
        floats(*own.shape),
        VMEM,
        after,
    )


def whole(refs):
    return jnp.concatenate([ref[...] for ref in refs], axis=1)


def edges_kernel(me_ref, *refs, streams, width):
    arrived, owns, olds = (refs[i * streams : (i + 1) * streams] for i in range(3))
    high_ref, low_ref, head_ref, tail_ref = refs[3 * streams :]
    trace = high_ref.shape[1] // 2
    first, last = slice(0, width), slice(trace - width, trace)
    passed = lax.rem(me_ref[0], 2) == 1

    def ends(ref):
        more = (slice(trace, trace + width), slice(2 * trace - width, 2 * trace))
        return jnp.concatenate([ref[:, cut] for cut in (first, last, *more)], axis=1)

    @pl.when(passed)
    def _():
        values = product(whole(arrived), ends(high_ref), ends(low_ref))
        own = whole(owns)
        for part, value in enumerate(values):
            head_ref[part] = value[:, :width] + own[part, :, first]
            tail_ref[part] = value[:, width:] + own[part, :, last]

    @pl.when(jnp.logical_not(passed))
    def _():
        old = whole(olds)
        head_ref[...] = old[:, :, first]
        tail_ref[...] = old[:, :, last]


def edges(me, arrived, panel, own, old, width, after):
    streams = len(own)
    shots = own[0].shape[1] * streams
    return call(
        lambda *refs: edges_kernel(*refs, streams=streams, width=width),
        "edges",
        [(SMEM, me)] + [(VMEM, value) for value in (*arrived, *own, *old, *panel)],
        [floats(2, shots, width)] * 2,
        [VMEM] * 2,
        after,
    )


def finish_kernel(me_ref, *refs, streams):
    arrived, owns, olds = (refs[i * streams : (i + 1) * streams] for i in range(3))
    high_ref, low_ref, out_ref, again_ref = refs[3 * streams :]
    passed = lax.rem(me_ref[0], 2) == 1

    @pl.when(passed)
    def _():
        real, imag = product(whole(arrived), high_ref[...], low_ref[...])
        own = whole(owns)
        out_ref[0] = real + own[0]
        out_ref[1] = imag + own[1]

    @pl.when(jnp.logical_not(passed))
    def _():
        out_ref[...] = whole(olds)

    again_ref[...] = out_ref[...]


def finish(me, arrived, panel, own, old, after):
    streams = len(own)
    _, rows, trace = own[0].shape
    return call(
        lambda *refs: finish_kernel(*refs, streams=streams),
        "finish",
        [(SMEM, me)] + [(VMEM, value) for value in (*arrived, *own, *old, *panel)],
        [floats(2, rows * streams, trace)] * 2,
        [VMEM] * 2,
        after,
    )


def middle_kernel(field_ref, high_ref, low_ref, forward_ref, out_ref, *, width):
    inner = slice(width, width + field_ref.shape[-1])
    real, imag = product(field_ref[...], high_ref[inner], low_ref[inner])
    total = forward_ref[0] * real + forward_ref[1] * imag
    out_ref[...] = jnp.sum(total, axis=0, keepdims=True)


def middle(field, maps, forward, width):
    return call(
        lambda *refs: middle_kernel(*refs, width=width),
        "middle",
        [(VMEM, value) for value in (field, *maps, forward)],
        floats(1, forward.shape[-1]),
        VMEM,
        (),
    )


def frame_kernel(high_ref, low_ref, high_out, low_out):
    width = high_out.shape[0] // 2
    depth = high_ref.shape[0]
    for ref, out in ((high_ref, high_out), (low_ref, low_out)):
        out[:width] = ref[:width]
        out[width:] = ref[depth - width :]


def frame(maps, width, after):
    shape = jax.ShapeDtypeStruct((2 * width, maps[0].shape[1]), jnp.bfloat16)
    return call(
        frame_kernel,
        "frame",
        [(VMEM, maps[0]), (VMEM, maps[1])],
        [shape] * 2,
        [VMEM] * 2,
        after,
    )


def model_kernel(arrived_ref, out_ref):
    out_ref[...] = jnp.sum(arrived_ref[...], axis=0)


def model_rows(arrived):
    return call(
        model_kernel, "model", [(VMEM, arrived)], floats(*arrived.shape[1:]), VMEM, ()
    )


def rim_kernel(rows_ref, part_ref, left_ref, right_ref, high_ref, low_ref, forward_ref, out_ref):
    shots, width = left_ref.shape[1], left_ref.shape[2]
    field = jnp.concatenate([left_ref[...], right_ref[...]], axis=-1)
    real, imag = product(field, high_ref[...], low_ref[...])
    total = forward_ref[0] * real + forward_ref[1] * imag
    gradient = part_ref[...] + jnp.sum(total, axis=0, keepdims=True)
    gradient = gradient * shots ** (-0.5)
    out_ref[...] = jnp.zeros_like(out_ref)
    for block in range(gradient.shape[1] // width):
        row = rows_ref[block]
        out_ref[pl.ds(row, 1), :] += gradient[:, block * width : (block + 1) * width]


def rim(rows, part, left, right, maps, forward, slabs):
    return call(
        rim_kernel,
        "rim",
        [(SMEM, rows)] + [(VMEM, value) for value in (part, left, right, *maps, forward)],
        floats(slabs * MBLK, left.shape[2]),
        VMEM,
        (),
    )


def body(
    residual_blocks,
    residual_slab,
    residual_pos,
    shot_ids,
    wavelet,
    down_panel,
    up_panel,
    recovery,
    forward_field,
    element_owner,
    element_slot,
):
    slabs = lax.axis_size("slab")
    lats = lax.axis_size("lat")
    groups = slabs // 2
    shots, width = residual_blocks.shape[2:]
    trace = down_panel.shape[-1]
    streams = 2 if shots % 32 == 0 else 1
    lanes = range(streams)
    rows = shots // streams
    me = lax.axis_index("slab").astype(jnp.int32).reshape(1)
    quads = slabs // 4
    sets = [(2, 0), (2, 1)] + [(4, quad) for quad in range(1, quads)]
    hops = quads.bit_length() - 1
    swapping = [(s, s ^ 1) for s in range(slabs)]

    def hop(value, route):
        return lax.ppermute(value, "slab", route)

    def toward(number, turn):
        size, which = sets[number]
        if turn == 0 and number != 1:
            return [(s, s ^ 2) for s in range(slabs)]
        bit = 1 << (turn if size == 2 else turn - 1)
        return [
            (s, s ^ (size * bit)) for s in range(slabs) if ((s // size) ^ which) & (2 * bit - 1) == bit
        ]

    def gather(which, after):
        return collect(
            me, residual_slab[:, 0], residual_pos, residual_blocks, which, trace, after
        )

    parts = gather(sets[:1], [])
    swapped = [hop(parts[0][1], swapping)]
    weights, targets = ready(shot_ids, element_owner[:, 0], element_slot, wavelet, [parts[0][0]])
    down = halves(down_panel[0, 0], [weights])
    parts += gather(sets[1:], [down[0]])
    total, sent, base = {}, {}, {}

    def stage_join(number, token):
        following = [part[1] for part in parts[number + 1 : number + 2]] if number >= 2 else []
        keep, joined, *gate = join(parts[number][0], swapped[number], following, token)
        total[number] = keep
        sent[number] = hop(joined, toward(number, 0))
        swapped.extend(hop(value, swapping) for value in gate)
        return [keep]

    def stage_add(number, turn, token):
        total[number] = add(total[number], sent[number], token)
        sent[number] = hop(total[number], toward(number, turn))
        return [total[number]]

    def stage_source(number, token):
        base[number] = source(total[number], sent[number], weights, token)
        return [base[number]]

    token = stage_join(0, [parts[1][0]])
    let = gate([part[1] for part in parts[1:3]], token)
    swapped += [hop(value, swapping) for value in let]
    token = let[:1]
    for turn in range(1, hops + 1):
        token = stage_add(0, turn, token)
    token = stage_join(1, token)
    up = halves(up_panel[0, 0], token)
    maps = halves(recovery[0, 0], [up[0]])
    rims = frame(maps, width, [])
    held = hold(me, 3, up_panel[0, 0], [rims[0]])
    far_panel = hop(held, [(p + 1, p) for p in range(2, slabs - 2, 2)])
    token = stage_source(0, [held])
    arrived = hop(base[0], [(0, 1)])
    for turn in range(1, hops + 1):
        token = stage_add(1, turn, token)
    token = stage_join(2, token)
    whole = step("down", me, 1, arrived, down, base[0], 0, base[0], token)
    arrived = [hop(whole, [(1, 2)])] * streams
    state = list(cleave(whole, streams, [whole]))
    token = stage_source(1, state[:1])
    for turn in range(1, hops + 1):
        token = stage_add(2, turn, token)
    held = hold(me, 1, up_panel[0, 0], token + arrived[:1])
    near_panel = hop(held, [(1, 0)])
    token = [held]
    for s in range(2, slabs):
        number = s // 2 if s < 4 else s // 4 + 1
        for t in lanes:
            state[t] = step("down", me, s, arrived[t], down, base[number], t * rows, state[t], token)
            token = [state[t]]
        if s + 1 < slabs:
            arrived = [hop(state[t], [(s, s + 1)]) for t in lanes]
        else:
            arrived = [hop(state[t], [(s, s - 1)]) for t in lanes]
            beside = [hop(state[t], [(p + 1, p) for p in range(0, slabs - 2, 2)]) for t in lanes]
        number = s // 4 + 2
        if number < len(sets):
            if s % 4 == 1:
                token = stage_join(number, token)
            if s % 4 == 2 and s > 2:
                for turn in range(1, hops + 1):
                    token = stage_add(number, turn, token)
            if s % 4 == 3:
                token = stage_source(number, token)
    above = list(state)
    for t in lanes:
        above[t] = step("up", me, slabs - 2, arrived[t], up, state[t], 0, above[t], token)
        token = [above[t]]
    arrived = [hop(above[t], [(slabs - 2, slabs - 4)]) for t in lanes]
    odd_up = halves_of_two(me, near_panel, far_panel, token)
    token = [odd_up[0]]
    for p in range(slabs - 4, -1, -2):
        if p == 0:
            after = [hop(above[t], [(q + 2, q + 1) for q in range(0, slabs - 2, 2)]) for t in lanes]
        for t in lanes:
            above[t] = up_step(
                me, p, arrived[t], odd_up, beside[t], up, state[t], above[t], token
            )
            token = [above[t]]
        if p > 0:
            arrived = [hop(above[t], [(p, p - 2)]) for t in lanes]
    head, tail = edges(me, after, up, state, above, width, token)
    left = lax.ppermute(tail, "lat", [(i, i + 1) for i in range(lats - 1)])
    right = lax.ppermute(head, "lat", [(i + 1, i) for i in range(lats - 1)])
    ups, field = finish(me, after, up, state, above, [head])
    part = middle(field, maps, forward_field[0, 0], width)
    outgoing = rim(targets, part, left, right, rims, forward_field[0, 0], slabs)
    arrived = lax.all_to_all(outgoing, "slab", split_axis=0, concat_axis=0, tiled=True)
    model = model_rows(arrived.reshape(slabs, MBLK, width))
    return (ups[None, None], model[None, None])


def solution(mesh):
    placed = (
        P(("slab", "lat"), None, None, None),
        P(("slab", "lat"), None),
        P(("slab", "lat")),
        P(),
        P(),
        P("slab", "lat", None, None, None),
        P("slab", "lat", None, None, None),
        P("slab", "lat", None, None, None),
        P("slab", "lat", None, None, None),
        P(("slab", "lat"), None),
        P(("slab", "lat")),
    )
    return jax.shard_map(
        body,
        mesh=mesh,
        in_specs=placed,
        out_specs=(P("slab", "lat", None, None, None), P("slab", "lat", None, None)),
        check_vma=False,
    )
```

```python
import jax
import jax.numpy as jnp
from jax import lax
from jax.experimental import pallas as pl
from jax.experimental.pallas import tpu as pltpu
from jax.sharding import PartitionSpec as P

MBLK = 8
VMEM = pl.BlockSpec(memory_space=pltpu.VMEM)
SMEM = pl.BlockSpec(memory_space=pltpu.SMEM)
ANY = pl.BlockSpec(memory_space=pl.ANY)
HBM = pl.BlockSpec(memory_space=pltpu.HBM)
CHUNKS = 4


def floats(*shape):
    return jax.ShapeDtypeStruct(shape, jnp.float32)


def cost(flops):
    return pl.CostEstimate(flops=flops, bytes_accessed=flops // 1000, transcendentals=0)


def split(value):
    high = value.astype(jnp.bfloat16)
    low = (value - high.astype(jnp.float32)).astype(jnp.bfloat16)
    return high, low


def product(vector, high, low):
    m, n = vector.shape[1], high.shape[1] // 2
    top, rest = split(vector.reshape(2 * m, -1))
    wide = jnp.dot(top, high, preferred_element_type=jnp.float32)
    wide += jnp.dot(rest, high, preferred_element_type=jnp.float32)
    wide += jnp.dot(top, low, preferred_element_type=jnp.float32)
    return wide[:m, :n] - wide[m:, n:], wide[:m, n:] + wide[m:, :n]


def call(kernel, name, ins, outs, out_specs, after, flops=0, room=16, **keywords):
    specs, values = zip(*ins)
    count = len(values)

    def run(*refs):
        kernel(*refs[:count], *refs[count + len(after) :])

    return pl.pallas_call(
        run,
        in_specs=list(specs) + [ANY] * len(after),
        out_specs=out_specs,
        out_shape=outs,
        compiler_params=pltpu.CompilerParams(vmem_limit_bytes=room * 1024 * 1024),
        cost_estimate=cost(flops) if flops else None,
        name=name,
        **keywords,
    )(*values, *after)


def halves_kernel(panel_ref, high_ref, low_ref):
    n = panel_ref.shape[-1]
    for part in range(2):
        high, low = split(panel_ref[part])
        high_ref[:, part * n : (part + 1) * n] = high
        low_ref[:, part * n : (part + 1) * n] = low


def halves(panel, after, rows=128):
    _, k, n = panel.shape
    block = pl.BlockSpec((rows, 2 * n), lambda i: (i, 0))
    return call(
        halves_kernel,
        "halves",
        [(pl.BlockSpec((2, rows, n), lambda i: (0, i, 0)), panel)],
        [jax.ShapeDtypeStruct((k, 2 * n), jnp.bfloat16)] * 2,
        [block, block],
        after,
        2 * 10**9,
        grid=(k // rows,),
    )


def either_kernel(me_ref, near_ref, far_ref, high_ref, low_ref):
    @pl.when(me_ref[0] < 2)
    def _():
        halves_kernel(near_ref, high_ref, low_ref)

    @pl.when(me_ref[0] >= 2)
    def _():
        halves_kernel(far_ref, high_ref, low_ref)


def halves_of_two(me, near, far, after, rows=128):
    _, k, n = near.shape
    piece = pl.BlockSpec((2, rows, n), lambda i: (0, i, 0))
    block = pl.BlockSpec((rows, 2 * n), lambda i: (i, 0))
    return call(
        either_kernel,
        "halves",
        [(SMEM, me), (piece, near), (piece, far)],
        [jax.ShapeDtypeStruct((k, 2 * n), jnp.bfloat16)] * 2,
        [block, block],
        after,
        grid=(k // rows,),
    )


def hold_kernel(me_ref, panel_ref, out_ref, *, least):
    slab = me_ref[0]

    @pl.when((lax.rem(slab, 2) == 1) & ((slab >= least) if least > 1 else (slab == least)))
    def _():
        out_ref[...] = panel_ref[...]


def hold(me, least, panel, after):
    return call(
        lambda *refs: hold_kernel(*refs, least=least),
        "hold",
        [(SMEM, me), (VMEM, panel)],
        floats(*panel.shape),
        VMEM,
        after,
    )


def collect_kernel(me_ref, slab_hbm, pos_hbm, blocks_hbm, *refs, sets):
    outs, (slab_ref, pos_ref, blocks_ref, sems) = refs[:-4], refs[-4:]
    count, width = blocks_ref.shape[0], blocks_ref.shape[-1]
    chunk = count // CHUNKS
    me = me_ref[0]
    copies = [
        pltpu.make_async_copy(slab_hbm, slab_ref, sems.at[CHUNKS]),
        pltpu.make_async_copy(pos_hbm, pos_ref, sems.at[CHUNKS + 1]),
    ]
    for i in range(CHUNKS):
        some = pl.ds(i * chunk, chunk)
        copies.append(pltpu.make_async_copy(blocks_hbm.at[some], blocks_ref.at[some], sems.at[i]))
    for copy in copies:
        copy.start()
    for out in outs:
        out[...] = jnp.zeros_like(out)
    copies[0].wait()
    copies[1].wait()

    def place(row, carry):
        slab = slab_ref[row]
        apart = lax.bitwise_xor(slab, me)
        side = lax.rem(apart, 2)
        lanes = pl.ds(pl.multiple_of(pos_ref[row] * width, width), width)
        for number, (size, which) in enumerate(sets):
            turn = lax.rem(lax.div(apart, 2), 2) if size == 4 else 0
            for other in range(2):

                @pl.when((lax.div(slab, size) == which) & (side == other))
                def _():
                    for part in range(2):
                        outs[2 * number + other][turn, part, :, lanes] += blocks_ref[row, part]

        return carry

    for i in range(CHUNKS):
        copies[2 + i].wait()
        lax.fori_loop(i * chunk, (i + 1) * chunk, place, 0)


def collect(me, slab, pos, blocks, sets, trace, after):
    shots = blocks.shape[2]
    shapes = [floats(size // 2, 2, shots, trace) for size, _ in sets for _ in range(2)]
    outs = call(
        lambda *refs: collect_kernel(*refs, sets=sets),
        "collect",
        [(SMEM, me), (HBM, slab), (HBM, pos), (HBM, blocks)],
        shapes,
        [VMEM] * len(shapes),
        after,
        2 * 10**9,
        59 if not after else 16,
        scratch_shapes=[
            pltpu.SMEM(slab.shape, jnp.int32),
            pltpu.SMEM(pos.shape, jnp.int32),
            pltpu.VMEM(blocks.shape, jnp.float32),
            pltpu.SemaphoreType.DMA((CHUNKS + 2,)),
        ],
    )
    return [outs[2 * i : 2 * i + 2] for i in range(len(sets))]


def ready_kernel(ids_ref, owner_ref, slot_ref, wavelet_ref, weights_ref, rows_ref):
    def pick(row, carry):
        weights_ref[pl.ds(row, 1), :] = wavelet_ref[pl.ds(ids_ref[row], 1), :]
        return carry

    lax.fori_loop(0, weights_ref.shape[0], pick, 0)

    def target(row, carry):
        rows_ref[row] = owner_ref[row] * MBLK + slot_ref[row]
        return carry

    lax.fori_loop(0, rows_ref.shape[0], target, 0)


def ready(ids, owner, slot, wavelet, after):
    return call(
        ready_kernel,
        "ready",
        [(SMEM, ids), (SMEM, owner), (SMEM, slot), (VMEM, wavelet)],
        [floats(*wavelet.shape), jax.ShapeDtypeStruct(slot.shape, jnp.int32)],
        [VMEM, SMEM],
        after,
    )


def join_kernel(mine_ref, arrived_ref, *refs, count):
    outs = refs[len(refs) - count :]
    last = mine_ref.shape[0] - 1
    outs[0][...] = mine_ref[0] + arrived_ref[0]
    outs[1][...] = mine_ref[last] + arrived_ref[last]
    if count == 3:
        outs[2][...] = refs[0][...]


def join(mine, arrived, following, after):
    count = 2 + len(following)
    return call(
        lambda *refs: join_kernel(*refs, count=count),
        "join",
        [(VMEM, value) for value in (mine, arrived, *following)],
        [floats(*mine.shape[1:])] * 2 + [floats(*value.shape) for value in following],
        [VMEM] * count,
        after,
    )


def gate_kernel(*refs):
    count = len(refs) // 2
    for value, out in zip(refs[:count], refs[count:]):
        out[...] = value[...]


def gate(values, after):
    return call(
        gate_kernel,
        "gate",
        [(VMEM, value) for value in values],
        [floats(*value.shape) for value in values],
        [VMEM] * len(values),
        after,
    )


def add_kernel(one_ref, two_ref, out_ref):
    out_ref[...] = one_ref[...] + two_ref[...]


def add(one, two, after):
    return call(add_kernel, "add", [(VMEM, one), (VMEM, two)], floats(*one.shape), VMEM, after)


def source_kernel(one_ref, two_ref, weights_ref, out_ref):
    weight_re, weight_im = weights_ref[:, 0:1], weights_ref[:, 1:2]
    real, imag = one_ref[0] + two_ref[0], one_ref[1] + two_ref[1]
    out_ref[0] = weight_re * real - weight_im * imag
    out_ref[1] = weight_re * imag + weight_im * real


def source(one, two, weights, after):
    return call(
        source_kernel,
        "source",
        [(VMEM, one), (VMEM, two), (VMEM, weights)],
        floats(*one.shape),
        VMEM,
        after,
    )


def cleave_kernel(field_ref, *outs):
    rows = outs[0].shape[1]
    for number, out in enumerate(outs):
        out[...] = field_ref[:, number * rows : (number + 1) * rows]


def cleave(field, streams, after):
    parts, shots, trace = field.shape
    return call(
        cleave_kernel,
        "cleave",
        [(VMEM, field)],
        [floats(parts, shots // streams, trace)] * streams,
        [VMEM] * streams,
        after,
    )


def step_kernel(me_ref, arrived_ref, high_ref, low_ref, own_ref, old_ref, out_ref, *, at, cut):
    active = me_ref[0] == at

    @pl.when(active)
    def _():
        arrived = arrived_ref[...] if arrived_ref.shape == out_ref.shape else arrived_ref[:, cut]
        real, imag = product(arrived, high_ref[...], low_ref[...])
        own = own_ref[...] if own_ref.shape == out_ref.shape else own_ref[:, cut]
        out_ref[0] = real + own[0]
        out_ref[1] = imag + own[1]

    @pl.when(jnp.logical_not(active))
    def _():
        out_ref[...] = old_ref[...]


def step(name, me, at, arrived, panel, own, first, old, after):
    cut = slice(first, first + old.shape[1])
    return call(
        lambda *refs: step_kernel(*refs, at=at, cut=cut),
        name,
        [(SMEM, me)] + [(VMEM, value) for value in (arrived, *panel, own, old)],
        floats(*old.shape),
        VMEM,
        after,
    )


def up_kernel(me_ref, arrived_ref, oh, ol, beside_ref, eh, el, own_ref, old_ref, out_ref, *, at):
    @pl.when(me_ref[0] == at)
    def _():
        real, imag = product(arrived_ref[...], oh[...], ol[...])
        out_ref[0] = real + beside_ref[0]
        out_ref[1] = imag + beside_ref[1]
        real, imag = product(out_ref[...], eh[...], el[...])
        out_ref[0] = real + own_ref[0]
        out_ref[1] = imag + own_ref[1]

    @pl.when(me_ref[0] != at)
    def _():
        out_ref[...] = old_ref[...]


def up_step(me, at, arrived, odd, beside, even, own, old, after):
    return call(
        lambda *refs: up_kernel(*refs, at=at),
        "up",
        [(SMEM, me)] + [(VMEM, value) for value in (arrived, *odd, beside, *even, own, old)],
        floats(*own.shape),
        VMEM,
        after,
    )


def whole(refs):
    return jnp.concatenate([ref[...] for ref in refs], axis=1)


def sides_kernel(high_ref, low_ref, high_out, low_out):
    trace = high_ref.shape[1] // 2
    width = high_out.shape[1] // 4
    for ref, out in ((high_ref, high_out), (low_ref, low_out)):
        for number, first in enumerate((0, trace - width, trace, 2 * trace - width)):
            out[:, number * width : (number + 1) * width] = ref[:, first : first + width]


def sides(panel, width, after):
    shape = jax.ShapeDtypeStruct((panel[0].shape[0], 4 * width), jnp.bfloat16)
    return call(
        sides_kernel,
        "sides",
        [(VMEM, panel[0]), (VMEM, panel[1])],
        [shape] * 2,
        [VMEM] * 2,
        after,
    )


def edges_kernel(me_ref, *refs, streams, width):
    arrived, owns, olds = (refs[i * streams : (i + 1) * streams] for i in range(3))
    high_ref, low_ref, head_ref, tail_ref = refs[3 * streams :]
    trace = owns[0].shape[-1]
    first, last = slice(0, width), slice(trace - width, trace)
    passed = lax.rem(me_ref[0], 2) == 1

    @pl.when(passed)
    def _():
        values = product(whole(arrived), high_ref[...], low_ref[...])
        own = whole(owns)
        for part, value in enumerate(values):
            head_ref[part] = value[:, :width] + own[part, :, first]
            tail_ref[part] = value[:, width:] + own[part, :, last]

    @pl.when(jnp.logical_not(passed))
    def _():
        old = whole(olds)
        head_ref[...] = old[:, :, first]
        tail_ref[...] = old[:, :, last]


def edges(me, arrived, panel, own, old, width, after):
    streams = len(own)
    shots = own[0].shape[1] * streams
    return call(
        lambda *refs: edges_kernel(*refs, streams=streams, width=width),
        "edges",
        [(SMEM, me)] + [(VMEM, value) for value in (*arrived, *own, *old, *panel)],
        [floats(2, shots, width)] * 2,
        [VMEM] * 2,
        after,
    )


def finish_kernel(me_ref, *refs, streams):
    arrived, owns, olds = (refs[i * streams : (i + 1) * streams] for i in range(3))
    high_ref, low_ref, out_ref, again_ref = refs[3 * streams :]
    passed = lax.rem(me_ref[0], 2) == 1

    @pl.when(passed)
    def _():
        real, imag = product(whole(arrived), high_ref[...], low_ref[...])
        own = whole(owns)
        out_ref[0] = real + own[0]
        out_ref[1] = imag + own[1]

    @pl.when(jnp.logical_not(passed))
    def _():
        out_ref[...] = whole(olds)

    again_ref[...] = out_ref[...]


def finish(me, arrived, panel, own, old, after):
    streams = len(own)
    _, rows, trace = own[0].shape
    return call(
        lambda *refs: finish_kernel(*refs, streams=streams),
        "finish",
        [(SMEM, me)] + [(VMEM, value) for value in (*arrived, *own, *old, *panel)],
        [floats(2, rows * streams, trace)] * 2,
        [VMEM] * 2,
        after,
    )


def middle_kernel(field_ref, high_ref, low_ref, forward_ref, out_ref, *, width):
    inner = slice(width, width + field_ref.shape[-1])
    real, imag = product(field_ref[...], high_ref[inner], low_ref[inner])
    total = forward_ref[0] * real + forward_ref[1] * imag
    out_ref[...] = jnp.sum(total, axis=0, keepdims=True)


def middle(field, maps, forward, width):
    return call(
        lambda *refs: middle_kernel(*refs, width=width),
        "middle",
        [(VMEM, value) for value in (field, *maps, forward)],
        floats(1, forward.shape[-1]),
        VMEM,
        (),
    )


def frame_kernel(high_ref, low_ref, high_out, low_out):
    width = high_out.shape[0] // 2
    depth = high_ref.shape[0]
    for ref, out in ((high_ref, high_out), (low_ref, low_out)):
        out[:width] = ref[:width]
        out[width:] = ref[depth - width :]


def frame(maps, width, after):
    shape = jax.ShapeDtypeStruct((2 * width, maps[0].shape[1]), jnp.bfloat16)
    return call(
        frame_kernel,
        "frame",
        [(VMEM, maps[0]), (VMEM, maps[1])],
        [shape] * 2,
        [VMEM] * 2,
        after,
    )


def model_kernel(arrived_ref, out_ref):
    out_ref[...] = jnp.sum(arrived_ref[...], axis=0)


def model_rows(arrived):
    return call(
        model_kernel, "model", [(VMEM, arrived)], floats(*arrived.shape[1:]), VMEM, ()
    )


def rim_kernel(rows_ref, part_ref, left_ref, right_ref, high_ref, low_ref, forward_ref, out_ref):
    shots, width = left_ref.shape[1], left_ref.shape[2]
    field = jnp.concatenate([left_ref[...], right_ref[...]], axis=-1)
    real, imag = product(field, high_ref[...], low_ref[...])
    total = forward_ref[0] * real + forward_ref[1] * imag
    gradient = part_ref[...] + jnp.sum(total, axis=0, keepdims=True)
    gradient = gradient * shots ** (-0.5)
    out_ref[...] = jnp.zeros_like(out_ref)
    for block in range(gradient.shape[1] // width):
        row = rows_ref[block]
        out_ref[pl.ds(row, 1), :] += gradient[:, block * width : (block + 1) * width]


def rim(rows, part, left, right, maps, forward, slabs):
    return call(
        rim_kernel,
        "rim",
        [(SMEM, rows)] + [(VMEM, value) for value in (part, left, right, *maps, forward)],
        floats(slabs * MBLK, left.shape[2]),
        VMEM,
        (),
    )


def body(
    residual_blocks,
    residual_slab,
    residual_pos,
    shot_ids,
    wavelet,
    down_panel,
    up_panel,
    recovery,
    forward_field,
    element_owner,
    element_slot,
):
    slabs = lax.axis_size("slab")
    lats = lax.axis_size("lat")
    groups = slabs // 2
    shots, width = residual_blocks.shape[2:]
    trace = down_panel.shape[-1]
    streams = 2 if shots % 32 == 0 else 1
    lanes = range(streams)
    rows = shots // streams
    me = lax.axis_index("slab").astype(jnp.int32).reshape(1)
    quads = slabs // 4
    sets = [(2, 0), (2, 1)] + [(4, quad) for quad in range(1, quads)]
    hops = quads.bit_length() - 1
    swapping = [(s, s ^ 1) for s in range(slabs)]

    def hop(value, route):
        return lax.ppermute(value, "slab", route)

    def toward(number, turn):
        size, which = sets[number]
        if turn == 0 and number != 1:
            return [(s, s ^ 2) for s in range(slabs)]
        bit = 1 << (turn if size == 2 else turn - 1)
        return [
            (s, s ^ (size * bit)) for s in range(slabs) if ((s // size) ^ which) & (2 * bit - 1) == bit
        ]

    def gather(which, after):
        return collect(
            me, residual_slab[:, 0], residual_pos, residual_blocks, which, trace, after
        )

    parts = gather(sets[:1], [])
    swapped = [hop(parts[0][1], swapping)]
    weights, targets = ready(shot_ids, element_owner[:, 0], element_slot, wavelet, [parts[0][0]])
    down = halves(down_panel[0, 0], [weights])
    parts += gather(sets[1:], [down[0]])
    total, sent, base = {}, {}, {}

    def stage_join(number, token):
        following = [part[1] for part in parts[number + 1 : number + 2]] if number >= 2 else []
        keep, joined, *gate = join(parts[number][0], swapped[number], following, token)
        total[number] = keep
        sent[number] = hop(joined, toward(number, 0))
        swapped.extend(hop(value, swapping) for value in gate)
        return [keep]

    def stage_add(number, turn, token):
        total[number] = add(total[number], sent[number], token)
        sent[number] = hop(total[number], toward(number, turn))
        return [total[number]]

    def stage_source(number, token):
        base[number] = source(total[number], sent[number], weights, token)
        return [base[number]]

    token = stage_join(0, [parts[1][0]])
    let = gate([part[1] for part in parts[1:3]], token)
    swapped += [hop(value, swapping) for value in let]
    token = let[:1]
    for turn in range(1, hops + 1):
        token = stage_add(0, turn, token)
    token = stage_join(1, token)
    up = halves(up_panel[0, 0], token)
    flanks = sides(up, width, [])
    maps = halves(recovery[0, 0], [flanks[0]])
    rims = frame(maps, width, [])
    held = hold(me, 3, up_panel[0, 0], [rims[0]])
    far_panel = hop(held, [(p + 1, p) for p in range(2, slabs - 2, 2)])
    token = stage_source(0, [held])
    arrived = hop(base[0], [(0, 1)])
    for turn in range(1, hops + 1):
        token = stage_add(1, turn, token)
    token = stage_join(2, token)
    whole = step("down", me, 1, arrived, down, base[0], 0, base[0], token)
    arrived = [hop(whole, [(1, 2)])] * streams
    state = list(cleave(whole, streams, [whole]))
    token = stage_source(1, state[:1])
    for turn in range(1, hops + 1):
        token = stage_add(2, turn, token)
    held = hold(me, 1, up_panel[0, 0], token + arrived[:1])
    near_panel = hop(held, [(1, 0)])
    token = [held]
    for s in range(2, slabs):
        number = s // 2 if s < 4 else s // 4 + 1
        for t in lanes:
            state[t] = step("down", me, s, arrived[t], down, base[number], t * rows, state[t], token)
            token = [state[t]]
        if s + 1 < slabs:
            arrived = [hop(state[t], [(s, s + 1)]) for t in lanes]
        else:
            arrived = [hop(state[t], [(s, s - 1)]) for t in lanes]
            beside = [hop(state[t], [(p + 1, p) for p in range(0, slabs - 2, 2)]) for t in lanes]
        number = s // 4 + 2
        if number < len(sets):
            if s % 4 == 1:
                token = stage_join(number, token)
            if s % 4 == 2 and s > 2:
                for turn in range(1, hops + 1):
                    token = stage_add(number, turn, token)
            if s % 4 == 3:
                token = stage_source(number, token)
    above = list(state)
    for t in lanes:
        above[t] = step("up", me, slabs - 2, arrived[t], up, state[t], 0, above[t], token)
        token = [above[t]]
    arrived = [hop(above[t], [(slabs - 2, slabs - 4)]) for t in lanes]
    odd_up = halves_of_two(me, near_panel, far_panel, token)
    token = [odd_up[0]]
    for p in range(slabs - 4, -1, -2):
        if p == 0:
            after = [hop(above[t], [(q + 2, q + 1) for q in range(0, slabs - 2, 2)]) for t in lanes]
        for t in lanes:
            above[t] = up_step(
                me, p, arrived[t], odd_up, beside[t], up, state[t], above[t], token
            )
            token = [above[t]]
        if p > 0:
            arrived = [hop(above[t], [(p, p - 2)]) for t in lanes]
    head, tail = edges(me, after, flanks, state, above, width, token)
    left = lax.ppermute(tail, "lat", [(i, i + 1) for i in range(lats - 1)])
    right = lax.ppermute(head, "lat", [(i + 1, i) for i in range(lats - 1)])
    ups, field = finish(me, after, up, state, above, [head])
    part = middle(field, maps, forward_field[0, 0], width)
    outgoing = rim(targets, part, left, right, rims, forward_field[0, 0], slabs)
    arrived = lax.all_to_all(outgoing, "slab", split_axis=0, concat_axis=0, tiled=True)
    model = model_rows(arrived.reshape(slabs, MBLK, width))
    return (ups[None, None], model[None, None])


def solution(mesh):
    placed = (
        P(("slab", "lat"), None, None, None),
        P(("slab", "lat"), None),
        P(("slab", "lat")),
        P(),
        P(),
        P("slab", "lat", None, None, None),
        P("slab", "lat", None, None, None),
        P("slab", "lat", None, None, None),
        P("slab", "lat", None, None, None),
        P(("slab", "lat"), None),
        P(("slab", "lat")),
    )
    return jax.shard_map(
        body,
        mesh=mesh,
        in_specs=placed,
        out_specs=(P("slab", "lat", None, None, None), P("slab", "lat", None, None)),
        check_vma=False,
    )
```
